32 devices in a mesh: flow: 8 (over z, x), cross: 4 (over y, core).
Axes of the slice: x: 2, y: 2, z: 4, core: 2. Of those that a mesh axis runs over, the one named last changes fastest.
Arguments:
- right_side: float32 [8, 256, 320], P('flow', 'cross'), may hold values from -6 to 6
- old_state: float32 [8, 256, 320], P('flow', 'cross'), may hold values from -6 to 6
- block_inverse: bfloat16 [8, 256, 320, 320], P('flow', 'cross'), as said below
- flux_jacobian: float32 [8, 256, 4, 25], P('flow', 'cross'), may hold values from -1.35 to 1.35, as said below
- face_lift: float32 [4, 64, 64], replicated, may hold values from -0.75 to 0.75
- upstream: int32 [8, 256], P('flow', 'cross'), may hold values from 0 to 255, as said below
- downstream: int32 [8, 256], P('flow', 'cross'), may hold values from 0 to 255, as said below
- live_counts: int32 [8, 4], P('flow', 'cross'), may hold values from 32 to 64, as said below
Outputs:
- half_sweep: float32 [8, 256, 320], P('flow', 'cross')
- full_sweep: float32 [8, 256, 320], P('flow', 'cross')
The draws below stay inside these ranges and needn't reach their ends.
Inputs may be any that keep to these rules, and one draw needn't show every extreme that they name: In each layer the upstream slots of an aligned block of 4 slots are a permutation of that same block's slots. downstream[l] is the inverse permutation of upstream[l + 1] (of upstream[0] for the last layer): upstream[l + 1, downstream[l, e]] = e. `live_counts`: slots at or beyond the count in their run hold no element; some run is full. `block_inverse`: each block is the sum of a multiple of the identity and a full dense part. `flux_jacobian`: entries are centred; those of the upstream and downstream faces are of order 0.45, those of the left and right faces of order 0.27.
All inputs are finite; a program needn't handle non-finite values.
Results may differ from the reference program's by a relative error of at most 0.017.
Values sent between devices are 32-bit elements; how exact they have to be, the bound alone decides.
A program may use at most 64 MiB of HBM per device.

```python
import math
import jax
import jax.numpy as jnp
from jax import lax

NVAR = 5
NB = 64
B = 320
E_DEV = 64
GRP = 4
LAYERS = 8
ELEMS = 256
N_CROSS = 4


def one_shuffle(block_key):
    return jax.random.permutation(block_key, GRP)


def neighbour_lists(key):
    block_total = LAYERS * ELEMS // GRP
    block_keys = jax.random.split(jax.random.fold_in(key, 71), block_total)
    shuffles = jax.vmap(one_shuffle)(block_keys).astype(jnp.int32)
    offsets = jnp.arange(block_total, dtype=jnp.int32) % (ELEMS // GRP) * GRP
    upward = (shuffles + offsets[:, None]).reshape(LAYERS, ELEMS)
    following = jnp.roll(upward, -1, axis=0)
    downward = jnp.argsort(following, axis=1, stable=True).astype(jnp.int32)
    return (upward, downward)


def draw_upstream(key, part):
    return neighbour_lists(key)[0]


def draw_downstream(key, part):
    return neighbour_lists(key)[1]


def draw_live_counts(key, part):
    lowest = max(1, E_DEV // 2)
    drawn = jax.random.randint(jax.random.fold_in(key, 5), (LAYERS, N_CROSS), lowest, E_DEV + 1, dtype=jnp.int32)
    spot_row = jax.random.randint(jax.random.fold_in(key, 6), (), 0, LAYERS, dtype=jnp.int32)
    spot_col = jax.random.randint(jax.random.fold_in(key, 7), (), 0, N_CROSS, dtype=jnp.int32)
    return drawn.at[spot_row, spot_col].set(E_DEV).astype(jnp.int32)


def draw_block_inverse(key, part):
    noise = jax.random.normal(jax.random.fold_in(key, 9), (LAYERS, ELEMS, B, B), jnp.float32)
    blocks = 0.85 * jnp.eye(B, dtype=jnp.float32) + 0.3 / math.sqrt(B) * noise
    return blocks.astype(jnp.bfloat16)


def draw_flux_jacobian(key, part):
    face_scale = jnp.array([1.0, 1.0, 0.6, 0.6], jnp.float32) / math.sqrt(5.0)
    shape = (LAYERS, ELEMS, 4, NVAR * NVAR)
    raw = jnp.clip(jax.random.normal(jax.random.fold_in(key, 11), shape, jnp.float32), -3.0, 3.0)
    return raw * face_scale[:, None]


def shard_levels(key, shape, cuts, least, top_value):
    def one(dim, parts):
        heights = jax.random.uniform(jax.random.fold_in(jax.random.fold_in(key, 6), dim), (parts,), jnp.float32, least / len(cuts), top_value / len(cuts))
        return jnp.repeat(jnp.exp(heights), shape[dim] // parts).reshape((-1,) + (1,) * (len(shape) - dim - 1))

    gain = one(*cuts[0])
    for cut in cuts[1:]:
        gain = gain * one(*cut)
    return gain


def gaussian(key, dims, width, bound, cuts=(), held_as=jnp.bfloat16):
    factor_of = shard_levels(key, dims, cuts, -0.22, 0.18) if cuts else 1.0
    result = jax.random.normal(key, dims, jnp.float32) * width * factor_of
    return jnp.minimum(jnp.maximum(result, -bound), bound).astype(held_as)


def setup_inputs(seed: int = 0) -> dict:
    seeds = jax.random.split(jax.random.key(seed), 9)
    right_side = gaussian(seeds[0], (LAYERS, ELEMS, B), 1.0, 6.0, ((0, 8), (1, 4)), jnp.float32)
    old_state = gaussian(seeds[1], (LAYERS, ELEMS, B), 1.0, 6.0, ((0, 8), (1, 4)), jnp.float32)
    block_inverse = draw_block_inverse(jax.random.fold_in(seeds[8], 71), 0)
    flux_jacobian = draw_flux_jacobian(jax.random.fold_in(seeds[8], 71), 0)
    face_lift = gaussian(seeds[4], (4, NB, NB), NB ** -0.5, 0.75, (), jnp.float32)
    upstream = draw_upstream(jax.random.fold_in(seeds[8], 71), 0)
    downstream = draw_downstream(jax.random.fold_in(seeds[8], 71), 0)
    live_counts = draw_live_counts(jax.random.fold_in(seeds[8], 71), 0)
    return dict(right_side=right_side, old_state=old_state, block_inverse=block_inverse, flux_jacobian=flux_jacobian, face_lift=face_lift, upstream=upstream, downstream=downstream, live_counts=live_counts)


HIGHEST_PRECISION = lax.Precision.HIGHEST


def couple(values, lift, jacobian_face):
    spread = jnp.einsum("...vc,bc->...vb", values, lift, precision=HIGHEST_PRECISION)
    mixing = jacobian_face.reshape(jacobian_face.shape[:-1] + (5, 5))
    return jnp.einsum("...uv,...vb->...ub", mixing, spread, precision=HIGHEST_PRECISION)


def solve_blocks(inverse, residual, live):
    flat = residual.reshape(residual.shape[:-2] + (-1,)).astype(jnp.bfloat16)
    flat = lax.optimization_barrier(flat).astype(jnp.float32)
    solved = jnp.einsum("...ij,...j->...i", inverse.astype(jnp.float32), flat, precision=HIGHEST_PRECISION)
    return (solved * live[..., None]).reshape(residual.shape)


def sideways(field):
    padded = jnp.pad(field, ((0, 0), (1, 1), (0, 0), (0, 0)))
    return padded[:, :-2], padded[:, 2:]


def reference(right_side, old_state, block_inverse, flux_jacobian, face_lift, upstream, downstream, live_counts):
    layer_count, elem_count, unknowns = right_side.shape
    grid_shape = (layer_count, elem_count, 5, unknowns // 5)
    source = right_side.reshape(grid_shape)
    slot_index = jnp.arange(elem_count, dtype=jnp.int32)
    owner_counts = live_counts[:, slot_index // E_DEV]
    live = (slot_index[None, :] % E_DEV < owner_counts).astype(jnp.float32)
    state_old = old_state.reshape(grid_shape) * live[:, :, None, None]
    left_old, right_old = sideways(state_old)
    following = jnp.concatenate([state_old[1:], jnp.zeros_like(state_old[:1])], 0)
    down_old = jnp.take_along_axis(following, downstream[:, :, None, None], axis=1)
    fixed_fwd = source - couple(down_old, face_lift[1], flux_jacobian[:, :, 1]) - couple(left_old, face_lift[2], flux_jacobian[:, :, 2]) - couple(right_old, face_lift[3], flux_jacobian[:, :, 3])

    def forward_step(previous, items):
        fixed_row, inverse_row, jacobian_row, up_row, live_row = items
        nearest = previous[up_row]
        solved = solve_blocks(inverse_row, fixed_row - couple(nearest, face_lift[0], jacobian_row[:, 0]), live_row)
        return solved, solved

    _, half_state = lax.scan(forward_step, jnp.zeros_like(source[0]), (fixed_fwd, block_inverse, flux_jacobian, upstream, live))
    left_half, right_half = sideways(half_state)
    earlier = jnp.concatenate([jnp.zeros_like(half_state[:1]), half_state[:-1]], 0)
    up_new = jnp.take_along_axis(earlier, upstream[:, :, None, None], axis=1)
    fixed_bwd = source - couple(up_new, face_lift[0], flux_jacobian[:, :, 0]) - couple(left_half, face_lift[2], flux_jacobian[:, :, 2]) - couple(right_half, face_lift[3], flux_jacobian[:, :, 3])

    def backward_step(later, items):
        fixed_row, inverse_row, jacobian_row, down_row, live_row = items
        nearest = later[down_row]
        solved = solve_blocks(inverse_row, fixed_row - couple(nearest, face_lift[1], jacobian_row[:, 1]), live_row)
        return solved, solved

    _, full_state = lax.scan(backward_step, jnp.zeros_like(source[0]), (fixed_bwd, block_inverse, flux_jacobian, downstream, live), reverse=True)
    return half_state.reshape(right_side.shape), full_state.reshape(right_side.shape)
```

```python
import functools

import jax
import jax.numpy as jnp
from jax import lax
from jax.experimental import pallas as pl
from jax.experimental.pallas import tpu as pltpu
from jax.sharding import PartitionSpec as P

NVAR = 5
GROUP = 8
MESH = pl.DeviceIdType.MESH
CONTRACT_LAST = (((1,), (1,)), ((), ()))


def sweep_kernel(
    nf, nc,
    rhs, old, ainv, jac, lift, up, down, cnt,
    half_out, full_out,
    a_vm, jx, lt, oldp, halfp, down_in, halo, fwd_in, bwd_in, fix_f, fix_b, rel,
    a_sem, old_send, old_recv, halo_send, halo_recv, fwd_send, fwd_recv, bwd_send, bwd_recv,
):
    elems, unk = rhs.shape[1], rhs.shape[2]
    nb = unk // NVAR
    wide = -(-unk // 128) * 128
    groups = elems // GROUP
    f = lax.axis_index("flow")
    c = lax.axis_index("cross")
    has_up, has_down = f > 0, f < nf - 1
    has_left, has_right = c > 0, c < nc - 1
    up_dev, down_dev = {"flow": f - 1}, {"flow": f + 1}
    left_dev, right_dev = {"cross": c - 1}, {"cross": c + 1}
    neighbours = ((has_up, up_dev), (has_down, down_dev), (has_left, left_dev), (has_right, right_dev))

    def rows(g):
        return pl.ds(pl.multiple_of(g * GROUP, GROUP), GROUP)

    def padded_rows(g):
        return pl.ds(pl.multiple_of(g * GROUP + GROUP, GROUP), GROUP)

    def a_copy(g):
        return pltpu.make_async_copy(ainv.at[0, rows(g)], a_vm.at[rows(g)], a_sem.at[g])

    def remote(src, dst, ssem, rsem, dev):
        return pltpu.make_async_remote_copy(
            src_ref=src, dst_ref=dst, send_sem=ssem, recv_sem=rsem,
            device_id=dev, device_id_type=MESH,
        )

    def old_copy():
        return remote(oldp.at[pl.ds(GROUP, elems)], down_in, old_send, old_recv, up_dev)

    def halo_copy(buf, which, slot, dev):
        start = elems if which == 0 else GROUP
        return remote(buf.at[pl.ds(start, GROUP)], halo.at[slot], halo_send.at[slot], halo_recv.at[slot], dev)

    def fwd_copy(g):
        return remote(halfp.at[padded_rows(g)], fwd_in.at[g], fwd_send.at[g], fwd_recv.at[g], down_dev)

    def bwd_copy(g):
        return remote(full_out.at[0, rows(g)], bwd_in.at[g], bwd_send.at[g], bwd_recv.at[g], up_dev)

    for g in range(groups):
        a_copy(g).start()

    barrier = pltpu.get_barrier_semaphore()
    for there, dev in neighbours:
        @pl.when(there)
        def _(dev=dev):
            pl.semaphore_signal(barrier, inc=1, device_id=dev, device_id_type=MESH)

    count = cnt[0, 0]
    slot = lax.broadcasted_iota(jnp.int32, (elems, unk), 0)
    oldp[pl.ds(GROUP, elems)] = jnp.where(slot < count, old[0], 0.0)

    pl.semaphore_wait(barrier, sum(there.astype(jnp.int32) for there, _ in neighbours))

    @pl.when(has_up)
    def _():
        old_copy().start()

    @pl.when(has_right)
    def _():
        halo_copy(oldp, 0, 0, right_dev).start()

    @pl.when(has_left)
    def _():
        halo_copy(oldp, 1, 1, left_dev).start()

    edge = jnp.zeros((GROUP, unk), jnp.float32)

    @pl.when(jnp.logical_not(has_up))
    def _():
        fwd_in[...] = jnp.zeros_like(fwd_in)

    @pl.when(jnp.logical_not(has_down))
    def _():
        down_in[...] = jnp.zeros_like(down_in)
        bwd_in[...] = jnp.zeros_like(bwd_in)

    @pl.when(jnp.logical_not(has_left))
    def _():
        halo[0] = edge
        halo[2] = edge

    @pl.when(jnp.logical_not(has_right))
    def _():
        halo[1] = edge
        halo[3] = edge

    square = (elems, elems)
    diagonal = lax.broadcasted_iota(jnp.int32, square, 0) == lax.broadcasted_iota(jnp.int32, square, 1)
    for i, index in enumerate((up, down)):
        local = (index[...] % GROUP).astype(jnp.float32)
        column = jnp.sum(jnp.where(diagonal, jnp.broadcast_to(local, square), 0.0), axis=1, keepdims=True)
        rel[i] = jnp.broadcast_to(column, (elems, 128))

    n2 = NVAR * NVAR
    entry = lax.broadcasted_iota(jnp.int32, (n2, NVAR * wide), 0)
    place = lax.broadcasted_iota(jnp.int32, (n2, NVAR * wide), 1)
    wanted = ((place % wide) // nb) * NVAR + place // wide
    spread_one = jnp.where(entry == wanted, 1.0, 0.0).astype(jnp.bfloat16)
    for d in range(4):
        block = lift[d].astype(jnp.bfloat16)
        lt[d] = jnp.concatenate([block] * NVAR, axis=0)
        values = jac[0, :, d, :]
        high = values.astype(jnp.bfloat16)
        low = (values - high.astype(jnp.float32)).astype(jnp.bfloat16)
        jx[d] = jnp.dot(high, spread_one, preferred_element_type=jnp.float32) + jnp.dot(
            low, spread_one, preferred_element_type=jnp.float32
        )

    def permuted(x, which, g):
        column = rel[which, rows(g)][:, 0:1]
        out = jnp.zeros_like(x)
        for k in range(GROUP):
            out = jnp.where(column == float(k), x[k : k + 1], out)
        return out

    def couple(x, d, where):
        n = x.shape[0]
        stacked = jnp.concatenate([x[:, v * nb : (v + 1) * nb] for v in range(NVAR)], axis=0)
        spread = lax.dot_general(
            stacked.astype(jnp.bfloat16), lt[d], CONTRACT_LAST, preferred_element_type=jnp.float32
        )
        total = None
        for v in range(NVAR):
            term = jx[d, where, v * wide : v * wide + unk] * spread[v * n : (v + 1) * n]
            total = term if total is None else total + term
        return total

    def solve(resid, g):
        flat = resid.astype(jnp.bfloat16)
        row = lax.broadcasted_iota(jnp.int32, (GROUP, unk), 0)
        out = jnp.zeros((GROUP, unk), jnp.float32)
        for k in range(GROUP):
            product = lax.dot_general(
                flat, a_vm[g * GROUP + k], CONTRACT_LAST, preferred_element_type=jnp.float32
            )
            out = jnp.where(row == k, product, out)
        return jnp.where(row + g * GROUP < count, out, 0.0)

    @pl.when(has_left)
    def _():
        halo_copy(oldp, 0, 0, right_dev).wait_recv()

    @pl.when(has_right)
    def _():
        halo_copy(oldp, 1, 1, left_dev).wait_recv()

    oldp[pl.ds(0, GROUP)] = halo[0]
    oldp[pl.ds(elems + GROUP, GROUP)] = halo[1]

    whole = pl.ds(0, elems)
    fix_f[...] = (
        rhs[0]
        - couple(oldp[pl.ds(GROUP - 1, elems)], 2, whole)
        - couple(oldp[pl.ds(GROUP + 1, elems)], 3, whole)
    )

    @pl.when(has_down)
    def _():
        old_copy().wait_recv()

    def arrange(g, carry):
        oldp[rows(g)] = permuted(down_in[rows(g)], 1, g)
        return carry

    @pl.when(has_up)
    def _():
        old_copy().wait_send()

    @pl.when(has_right)
    def _():
        halo_copy(oldp, 0, 0, right_dev).wait_send()

    @pl.when(has_left)
    def _():
        halo_copy(oldp, 1, 1, left_dev).wait_send()

    lax.fori_loop(0, groups, arrange, 0)
    fix_f[...] = fix_f[...] - couple(oldp[pl.ds(0, elems)], 1, whole)

    def forward(g, carry):
        a_copy(g).wait()

        @pl.when(has_up)
        def _():
            fwd_copy(g).wait_recv()

        coupled = couple(permuted(fwd_in[g], 0, g), 0, rows(g))
        fix_b[rows(g)] = rhs[0, rows(g)] - coupled
        solved = solve(fix_f[rows(g)] - coupled, g)
        halfp[padded_rows(g)] = solved

        @pl.when(has_down)
        def _():
            fwd_copy(g).start()

        half_out[0, rows(g)] = solved

        @pl.when(jnp.logical_and(g == 0, has_left))
        def _():
            halo_copy(halfp, 1, 3, left_dev).start()

        return carry

    lax.fori_loop(0, groups, forward, 0)

    @pl.when(has_right)
    def _():
        halo_copy(halfp, 0, 2, right_dev).start()
        halo_copy(halfp, 1, 3, left_dev).wait_recv()

    @pl.when(has_left)
    def _():
        halo_copy(halfp, 0, 2, right_dev).wait_recv()

    halfp[pl.ds(0, GROUP)] = halo[2]
    halfp[pl.ds(elems + GROUP, GROUP)] = halo[3]
    fix_b[...] = (
        fix_b[...]
        - couple(halfp[pl.ds(GROUP - 1, elems)], 2, whole)
        - couple(halfp[pl.ds(GROUP + 1, elems)], 3, whole)
    )

    def backward(i, carry):
        g = groups - 1 - i

        @pl.when(has_down)
        def _():
            bwd_copy(g).wait_recv()

        coupled = couple(permuted(bwd_in[g], 1, g), 1, rows(g))
        full_out[0, rows(g)] = solve(fix_b[rows(g)] - coupled, g)

        @pl.when(has_up)
        def _():
            bwd_copy(g).start()

        return carry

    lax.fori_loop(0, groups, backward, 0)

    def drain(g, carry):
        @pl.when(has_down)
        def _():
            fwd_copy(g).wait_send()

        @pl.when(has_up)
        def _():
            bwd_copy(g).wait_send()

        return carry

    lax.fori_loop(0, groups, drain, 0)

    @pl.when(has_right)
    def _():
        halo_copy(halfp, 0, 2, right_dev).wait_send()

    @pl.when(has_left)
    def _():
        halo_copy(halfp, 1, 3, left_dev).wait_send()


def per_device(
    right_side, old_state, block_inverse, flux_jacobian, face_lift, upstream, downstream, live_counts
):
    layers, elems, unk = right_side.shape
    assert layers == 1 and elems % GROUP == 0
    nf, nc = lax.axis_size("flow"), lax.axis_size("cross")
    nb = unk // NVAR
    wide = -(-unk // 128) * 128
    groups = elems // GROUP
    vmem = pl.BlockSpec(memory_space=pltpu.VMEM)
    f32 = jnp.float32
    dma = pltpu.SemaphoreType.DMA
    return pl.pallas_call(
        functools.partial(sweep_kernel, nf, nc),
        out_shape=(jax.ShapeDtypeStruct(right_side.shape, f32),) * 2,
        in_specs=[
            vmem, vmem, pl.BlockSpec(memory_space=pl.ANY), vmem, vmem, vmem, vmem,
            pl.BlockSpec(memory_space=pltpu.SMEM),
        ],
        out_specs=(vmem, vmem),
        scratch_shapes=[
            pltpu.VMEM((elems, unk, unk), jnp.bfloat16),
            pltpu.VMEM((4, elems, NVAR * wide), f32),
            pltpu.VMEM((4, unk, nb), jnp.bfloat16),
            pltpu.VMEM((elems + 2 * GROUP, unk), f32),
            pltpu.VMEM((elems + 2 * GROUP, unk), f32),
            pltpu.VMEM((elems, unk), f32),
            pltpu.VMEM((4, GROUP, unk), f32),
            pltpu.VMEM((groups, GROUP, unk), f32),
            pltpu.VMEM((groups, GROUP, unk), f32),
            pltpu.VMEM((elems, unk), f32),
            pltpu.VMEM((elems, unk), f32),
            pltpu.VMEM((2, elems, 128), f32),
            dma((groups,)), dma, dma, dma((4,)), dma((4,)),
            dma((groups,)), dma((groups,)), dma((groups,)), dma((groups,)),
        ],
        compiler_params=pltpu.CompilerParams(
            collective_id=0, has_side_effects=True, vmem_limit_bytes=40 * 1024 * 1024
        ),
        cost_estimate=pl.CostEstimate(
            flops=4 * elems * unk * unk, bytes_accessed=2 * elems * unk * unk, transcendentals=0
        ),
        name="sweep",
    )(right_side, old_state, block_inverse, flux_jacobian, face_lift, upstream, downstream, live_counts)


def solution(mesh):
    in_specs = (
        P("flow", "cross", None),
        P("flow", "cross", None),
        P("flow", "cross", None, None),
        P("flow", "cross", None, None),
        P(),
        P("flow", "cross"),
        P("flow", "cross"),
        P("flow", "cross"),
    )
    out_specs = (P("flow", "cross", None), P("flow", "cross", None))
    return jax.shard_map(
        per_device, mesh=mesh, in_specs=in_specs, out_specs=out_specs, check_vma=False
    )
```

```python
import functools

import jax
import jax.numpy as jnp
from jax import lax
from jax.experimental import pallas as pl
from jax.experimental.pallas import tpu as pltpu
from jax.sharding import PartitionSpec as P

NVAR = 5
GROUP = 8
BLOCK = 4
VMEM_BYTES = 64 * 1024 * 1024
MESH = pl.DeviceIdType.MESH
CONTRACT_LAST = (((1,), (1,)), ((), ()))
CONTRACT_FIRST = (((0,), (0,)), ((), ()))


def sweep_kernel(
    nf, nc,
    rhs_hbm, old_hbm, ainv, jac_hbm, lift_hbm, up_hbm, down_hbm, cnt_hbm,
    half_out, full_out,
    rhs, old, jac, lift, up, down, cnt,
    a_vm, jx, lt, oldp, halfp, down_in, halo, fwd_in, bwd_in, fwd_snd, bwd_snd, fix_f, fix_b, rel,
    in_sem, a_sem, old_send, old_recv, halo_send, halo_recv, fwd_send, fwd_recv, bwd_send, bwd_recv,
):
    elems, unk = rhs.shape[1], rhs.shape[2]
    halves = GROUP // BLOCK
    nb = unk // NVAR
    wide = -(-unk // 128) * 128
    groups = elems // GROUP
    f = lax.axis_index("flow")
    c = lax.axis_index("cross")
    has_up, has_down = f > 0, f < nf - 1
    has_left, has_right = c > 0, c < nc - 1
    up_dev, down_dev = {"flow": f - 1}, {"flow": f + 1}
    left_dev, right_dev = {"cross": c - 1}, {"cross": c + 1}
    neighbours = ((has_up, up_dev), (has_down, down_dev), (has_left, left_dev), (has_right, right_dev))

    def rows(g):
        return pl.ds(pl.multiple_of(g * GROUP, GROUP), GROUP)

    def padded_rows(g):
        return pl.ds(pl.multiple_of(g * GROUP + GROUP, GROUP), GROUP)

    def a_copy(g):
        return pltpu.make_async_copy(ainv.at[0, rows(g)], a_vm.at[rows(g)], a_sem.at[g])

    def remote(src, dst, ssem, rsem, dev):
        return pltpu.make_async_remote_copy(
            src_ref=src, dst_ref=dst, send_sem=ssem, recv_sem=rsem,
            device_id=dev, device_id_type=MESH,
        )

    def old_copy():
        return remote(oldp.at[pl.ds(GROUP, elems)], down_in, old_send, old_recv, up_dev)

    def halo_copy(buf, which, slot, dev):
        start = elems if which == 0 else GROUP
        return remote(buf.at[pl.ds(start, GROUP)], halo.at[slot], halo_send.at[slot], halo_recv.at[slot], dev)

    def fwd_copy(g):
        return remote(fwd_snd.at[g], fwd_in.at[g], fwd_send.at[g], fwd_recv.at[g], down_dev)

    def bwd_copy(g):
        return remote(bwd_snd.at[g], bwd_in.at[g], bwd_send.at[g], bwd_recv.at[g], up_dev)

    sources = (old_hbm, cnt_hbm, jac_hbm, lift_hbm, up_hbm, down_hbm, rhs_hbm)
    fetches = [
        pltpu.make_async_copy(src, dst, in_sem.at[i])
        for i, (src, dst) in enumerate(zip(sources, (old, cnt, jac, lift, up, down, rhs)))
    ]
    for fetch in fetches:
        fetch.start()
    for g in range(groups):
        a_copy(g).start()

    barrier = pltpu.get_barrier_semaphore()
    for there, dev in neighbours:
        @pl.when(there)
        def _(dev=dev):
            pl.semaphore_signal(barrier, inc=1, device_id=dev, device_id_type=MESH)

    fetches[0].wait()
    fetches[1].wait()
    count = cnt[...]
    slot = lax.broadcasted_iota(jnp.int32, (elems, unk), 0)
    oldp[pl.ds(GROUP, elems)] = jnp.where(slot < count, old[0], 0.0)

    pl.semaphore_wait(barrier, sum(there.astype(jnp.int32) for there, _ in neighbours))

    @pl.when(has_up)
    def _():
        old_copy().start()

    @pl.when(has_right)
    def _():
        halo_copy(oldp, 0, 0, right_dev).start()

    @pl.when(has_left)
    def _():
        halo_copy(oldp, 1, 1, left_dev).start()

    edge = jnp.zeros((GROUP, unk), jnp.float32)

    @pl.when(jnp.logical_not(has_up))
    def _():
        fwd_in[...] = jnp.zeros_like(fwd_in)

    @pl.when(jnp.logical_not(has_down))
    def _():
        down_in[...] = jnp.zeros_like(down_in)
        bwd_in[...] = jnp.zeros_like(bwd_in)

    @pl.when(jnp.logical_not(has_left))
    def _():
        halo[0] = edge
        halo[2] = edge

    @pl.when(jnp.logical_not(has_right))
    def _():
        halo[1] = edge
        halo[3] = edge

    for fetch in fetches[2:]:
        fetch.wait()

    square = (elems, elems)
    diagonal = lax.broadcasted_iota(jnp.int32, square, 0) == lax.broadcasted_iota(jnp.int32, square, 1)
    for i, index in enumerate((up, down)):
        local = (index[...] % BLOCK).astype(jnp.float32)
        column = jnp.sum(jnp.where(diagonal, jnp.broadcast_to(local, square), 0.0), axis=1, keepdims=True)
        rel[i] = jnp.broadcast_to(column, (elems, 128))

    n2 = NVAR * NVAR
    entry = lax.broadcasted_iota(jnp.int32, (n2, NVAR * wide), 0)
    place = lax.broadcasted_iota(jnp.int32, (n2, NVAR * wide), 1)
    wanted = ((place % wide) // nb) * NVAR + place // wide
    spread_one = jnp.where(entry == wanted, 1.0, 0.0).astype(jnp.bfloat16)
    for d in range(4):
        block = lift[d].astype(jnp.bfloat16)
        lt[d] = jnp.concatenate([block] * NVAR, axis=0)
        values = jac[:, d, :]
        high = values.astype(jnp.bfloat16)
        low = (values - high.astype(jnp.float32)).astype(jnp.bfloat16)
        jx[d] = lax.dot_general(
            high, spread_one, CONTRACT_FIRST, preferred_element_type=jnp.float32
        ) + lax.dot_general(low, spread_one, CONTRACT_FIRST, preferred_element_type=jnp.float32)

    row = lax.broadcasted_iota(jnp.int32, (GROUP, unk), 0)

    def permuted(x, which, g):
        column = rel[which, rows(g)][:, 0:1]
        out = jnp.broadcast_to(x[0:1], (GROUP, unk))
        for k in range(1, BLOCK):
            out = jnp.where(column == float(k), x[k : k + 1], out)
        return out

    def couple(x, d, where):
        n = x.shape[0]
        stacked = jnp.concatenate([x[:, v * nb : (v + 1) * nb] for v in range(NVAR)], axis=0)
        spread = lax.dot_general(
            stacked.astype(jnp.bfloat16), lt[d], CONTRACT_LAST, preferred_element_type=jnp.float32
        )
        total = None
        for v in range(NVAR):
            term = jx[d, where, v * wide : v * wide + unk] * spread[v * n : (v + 1) * n]
            total = term if total is None else total + term
        return total

    def solve(resid, g, h):
        flat = resid.astype(jnp.bfloat16)
        out = jnp.zeros((GROUP, unk), jnp.float32)
        for k in range(h * BLOCK, (h + 1) * BLOCK):
            product = lax.dot_general(
                flat, a_vm[g * GROUP + k], CONTRACT_LAST, preferred_element_type=jnp.float32
            )
            out = jnp.where(row == k, product, out)
        return jnp.where(row + g * GROUP < count, out, 0.0)

    @pl.when(has_left)
    def _():
        halo_copy(oldp, 0, 0, right_dev).wait_recv()

    @pl.when(has_right)
    def _():
        halo_copy(oldp, 1, 1, left_dev).wait_recv()

    oldp[pl.ds(0, GROUP)] = halo[0]
    oldp[pl.ds(elems + GROUP, GROUP)] = halo[1]

    whole = pl.ds(0, elems)
    fix_f[...] = (
        rhs[0]
        - couple(oldp[pl.ds(GROUP - 1, elems)], 2, whole)
        - couple(oldp[pl.ds(GROUP + 1, elems)], 3, whole)
    )

    @pl.when(has_down)
    def _():
        old_copy().wait_recv()

    def arrange(g, carry):
        x = down_in[rows(g)]
        oldp[rows(g)] = jnp.where(row < BLOCK, permuted(x[:BLOCK], 1, g), permuted(x[BLOCK:], 1, g))
        return carry

    @pl.when(has_up)
    def _():
        old_copy().wait_send()

    @pl.when(has_right)
    def _():
        halo_copy(oldp, 0, 0, right_dev).wait_send()

    @pl.when(has_left)
    def _():
        halo_copy(oldp, 1, 1, left_dev).wait_send()

    lax.fori_loop(0, groups, arrange, 0)
    fix_f[...] = fix_f[...] - couple(oldp[pl.ds(0, elems)], 1, whole)

    def forward(g, carry):
        a_copy(g).wait()

        fixed = fix_f[rows(g)]
        coupling = jnp.zeros((GROUP, unk), jnp.float32)
        result = jnp.zeros((GROUP, unk), jnp.float32)
        for h in range(halves):
            j = g * halves + h

            @pl.when(has_up)
            def _():
                fwd_copy(j).wait_recv()

            coupled = couple(permuted(fwd_in[j], 0, g), 0, rows(g))
            solved = solve(fixed - coupled, g, h)
            fwd_snd[j] = solved[h * BLOCK : (h + 1) * BLOCK]

            @pl.when(has_down)
            def _():
                fwd_copy(j).start()

            coupling = jnp.where(row // BLOCK == h, coupled, coupling)
            result = result + solved
        fix_b[rows(g)] = rhs[0, rows(g)] - coupling
        halfp[padded_rows(g)] = result
        half_out[0, rows(g)] = result

        @pl.when(jnp.logical_and(g == 0, has_left))
        def _():
            halo_copy(halfp, 1, 3, left_dev).start()

        return carry

    lax.fori_loop(0, groups, forward, 0)

    @pl.when(has_right)
    def _():
        halo_copy(halfp, 0, 2, right_dev).start()
        halo_copy(halfp, 1, 3, left_dev).wait_recv()

    @pl.when(has_left)
    def _():
        halo_copy(halfp, 0, 2, right_dev).wait_recv()

    halfp[pl.ds(0, GROUP)] = halo[2]
    halfp[pl.ds(elems + GROUP, GROUP)] = halo[3]
    fix_b[...] = (
        fix_b[...]
        - couple(halfp[pl.ds(GROUP - 1, elems)], 2, whole)
        - couple(halfp[pl.ds(GROUP + 1, elems)], 3, whole)
    )

    def backward(i, carry):
        g = groups - 1 - i

        fixed = fix_b[rows(g)]
        result = jnp.zeros((GROUP, unk), jnp.float32)
        for h in reversed(range(halves)):
            j = g * halves + h

            @pl.when(has_down)
            def _():
                bwd_copy(j).wait_recv()

            coupled = couple(permuted(bwd_in[j], 1, g), 1, rows(g))
            solved = solve(fixed - coupled, g, h)
            bwd_snd[j] = solved[h * BLOCK : (h + 1) * BLOCK]

            @pl.when(has_up)
            def _():
                bwd_copy(j).start()

            result = result + solved
        full_out[0, rows(g)] = result
        return carry

    lax.fori_loop(0, groups, backward, 0)

    def drain(g, carry):
        @pl.when(has_down)
        def _():
            fwd_copy(g).wait_send()

        @pl.when(has_up)
        def _():
            bwd_copy(g).wait_send()

        return carry

    lax.fori_loop(0, groups * halves, drain, 0)

    @pl.when(has_right)
    def _():
        halo_copy(halfp, 0, 2, right_dev).wait_send()

    @pl.when(has_left)
    def _():
        halo_copy(halfp, 1, 3, left_dev).wait_send()


def per_device(
    right_side, old_state, block_inverse, flux_jacobian, face_lift, upstream, downstream, live_counts
):
    layers, elems, unk = right_side.shape
    assert layers == 1 and elems % GROUP == 0
    nf, nc = lax.axis_size("flow"), lax.axis_size("cross")
    nb = unk // NVAR
    wide = -(-unk // 128) * 128
    groups = elems // GROUP
    vmem = pl.BlockSpec(memory_space=pltpu.VMEM)
    hbm = pl.BlockSpec(memory_space=pltpu.HBM)
    blocks = elems // BLOCK
    jacobian = jnp.transpose(flux_jacobian[0], (2, 1, 0))
    f32 = jnp.float32
    dma = pltpu.SemaphoreType.DMA
    return pl.pallas_call(
        functools.partial(sweep_kernel, nf, nc),
        out_shape=(jax.ShapeDtypeStruct(right_side.shape, f32),) * 2,
        in_specs=[
            hbm, hbm, hbm, hbm, hbm, hbm, hbm, hbm,
        ],
        out_specs=(vmem, vmem),
        scratch_shapes=[
            pltpu.VMEM(right_side.shape, f32),
            pltpu.VMEM(old_state.shape, f32),
            pltpu.VMEM(jacobian.shape, f32),
            pltpu.VMEM(face_lift.shape, f32),
            pltpu.VMEM(upstream.shape, jnp.int32),
            pltpu.VMEM(downstream.shape, jnp.int32),
            pltpu.VMEM(live_counts.shape, jnp.int32),
            pltpu.VMEM((elems, unk, unk), jnp.bfloat16),
            pltpu.VMEM((4, elems, NVAR * wide), f32),
            pltpu.VMEM((4, unk, nb), jnp.bfloat16),
            pltpu.VMEM((elems + 2 * GROUP, unk), f32),
            pltpu.VMEM((elems + 2 * GROUP, unk), f32),
            pltpu.VMEM((elems, unk), f32),
            pltpu.VMEM((4, GROUP, unk), f32),
            pltpu.VMEM((blocks, BLOCK, unk), f32),
            pltpu.VMEM((blocks, BLOCK, unk), f32),
            pltpu.VMEM((blocks, BLOCK, unk), f32),
            pltpu.VMEM((blocks, BLOCK, unk), f32),
            pltpu.VMEM((elems, unk), f32),
            pltpu.VMEM((elems, unk), f32),
            pltpu.VMEM((2, elems, 128), f32),
            dma((7,)), dma((groups,)), dma, dma, dma((4,)), dma((4,)),
            dma((blocks,)), dma((blocks,)), dma((blocks,)), dma((blocks,)),
        ],
        compiler_params=pltpu.CompilerParams(
            collective_id=0, has_side_effects=True, vmem_limit_bytes=VMEM_BYTES
        ),
        cost_estimate=pl.CostEstimate(
            flops=4 * elems * unk * unk, bytes_accessed=2 * elems * unk * unk, transcendentals=0
        ),
        name="sweep",
    )(right_side, old_state, block_inverse, jacobian, face_lift, upstream, downstream, live_counts)


def solution(mesh):
    in_specs = (
        P("flow", "cross", None),
        P("flow", "cross", None),
        P("flow", "cross", None, None),
        P("flow", "cross", None, None),
        P(),
        P("flow", "cross"),
        P("flow", "cross"),
        P("flow", "cross"),
    )
    out_specs = (P("flow", "cross", None), P("flow", "cross", None))
    return jax.shard_map(
        per_device, mesh=mesh, in_specs=in_specs, out_specs=out_specs, check_vma=False
    )
```

```python
import functools

import jax
import jax.numpy as jnp
from jax import lax
from jax.experimental import pallas as pl
from jax.experimental.pallas import tpu as pltpu
from jax.sharding import PartitionSpec as P

NVAR = 5
GROUP = 8
BLOCK = 4
VMEM_BYTES = 64 * 1024 * 1024
MESH = pl.DeviceIdType.MESH
CONTRACT_LAST = (((1,), (1,)), ((), ()))
CONTRACT_FIRST = (((0,), (0,)), ((), ()))


def sweep_kernel(
    nf, nc,
    rhs_hbm, old_hbm, ainv, jac_hbm, lift_hbm, up_hbm, down_hbm, cnt_hbm,
    half_out, full_out,
    rhs, old, jac, lift, up, down, cnt,
    a_vm, jx, lt, oldp, halfp, down_in, halo, fwd_in, bwd_in, fwd_snd, bwd_snd, fix_f, fix_b, rel,
    in_sem, a_sem, old_send, old_recv, halo_send, halo_recv, fwd_send, fwd_recv, bwd_send, bwd_recv,
):
    elems, unk = rhs.shape[1], rhs.shape[2]
    halves = GROUP // BLOCK
    nb = unk // NVAR
    wide = -(-unk // 128) * 128
    groups = elems // GROUP
    f = lax.axis_index("flow")
    c = lax.axis_index("cross")
    has_up, has_down = f > 0, f < nf - 1
    has_left, has_right = c > 0, c < nc - 1
    up_dev, down_dev = {"flow": f - 1}, {"flow": f + 1}
    left_dev, right_dev = {"cross": c - 1}, {"cross": c + 1}
    neighbours = ((has_up, up_dev), (has_down, down_dev), (has_left, left_dev), (has_right, right_dev))

    def rows(g):
        return pl.ds(pl.multiple_of(g * GROUP, GROUP), GROUP)

    def padded_rows(g):
        return pl.ds(pl.multiple_of(g * GROUP + GROUP, GROUP), GROUP)

    def a_copy(g):
        return pltpu.make_async_copy(ainv.at[0, rows(g)], a_vm.at[rows(g)], a_sem.at[g])

    def remote(src, dst, ssem, rsem, dev):
        return pltpu.make_async_remote_copy(
            src_ref=src, dst_ref=dst, send_sem=ssem, recv_sem=rsem,
            device_id=dev, device_id_type=MESH,
        )

    def old_copy():
        return remote(oldp.at[pl.ds(GROUP, elems)], down_in, old_send, old_recv, up_dev)

    def halo_copy(buf, which, slot, dev):
        start = elems if which == 0 else GROUP
        return remote(buf.at[pl.ds(start, GROUP)], halo.at[slot], halo_send.at[slot], halo_recv.at[slot], dev)

    def fwd_copy(g):
        return remote(fwd_snd.at[g], fwd_in.at[g], fwd_send.at[g], fwd_recv.at[g], down_dev)

    def bwd_copy(g):
        return remote(bwd_snd.at[g], bwd_in.at[g], bwd_send.at[g], bwd_recv.at[g], up_dev)

    sources = (old_hbm, cnt_hbm, jac_hbm, lift_hbm, up_hbm, down_hbm, rhs_hbm)
    fetches = [
        pltpu.make_async_copy(src, dst, in_sem.at[i])
        for i, (src, dst) in enumerate(zip(sources, (old, cnt, jac, lift, up, down, rhs)))
    ]
    for fetch in fetches:
        fetch.start()
    for g in range(groups):
        a_copy(g).start()

    barrier = pltpu.get_barrier_semaphore()
    for there, dev in neighbours:
        @pl.when(there)
        def _(dev=dev):
            pl.semaphore_signal(barrier, inc=1, device_id=dev, device_id_type=MESH)

    fetches[0].wait()
    fetches[1].wait()
    count = cnt[...]
    slot = lax.broadcasted_iota(jnp.int32, (elems, unk), 0)
    oldp[pl.ds(GROUP, elems)] = jnp.where(slot < count, old[0], 0.0)

    pl.semaphore_wait(barrier, sum(there.astype(jnp.int32) for there, _ in neighbours))

    @pl.when(has_up)
    def _():
        old_copy().start()

    @pl.when(has_right)
    def _():
        halo_copy(oldp, 0, 0, right_dev).start()

    @pl.when(has_left)
    def _():
        halo_copy(oldp, 1, 1, left_dev).start()

    edge = jnp.zeros((GROUP, unk), jnp.float32)

    @pl.when(jnp.logical_not(has_up))
    def _():
        fwd_in[...] = jnp.zeros_like(fwd_in)

    @pl.when(jnp.logical_not(has_down))
    def _():
        down_in[...] = jnp.zeros_like(down_in)
        bwd_in[...] = jnp.zeros_like(bwd_in)

    @pl.when(jnp.logical_not(has_left))
    def _():
        halo[0] = edge
        halo[2] = edge

    @pl.when(jnp.logical_not(has_right))
    def _():
        halo[1] = edge
        halo[3] = edge

    for fetch in fetches[2:]:
        fetch.wait()

    square = (elems, elems)
    diagonal = lax.broadcasted_iota(jnp.int32, square, 0) == lax.broadcasted_iota(jnp.int32, square, 1)
    for i, index in enumerate((up, down)):
        local = (index[...] % BLOCK).astype(jnp.float32)
        column = jnp.sum(jnp.where(diagonal, jnp.broadcast_to(local, square), 0.0), axis=1, keepdims=True)
        rel[i] = jnp.broadcast_to(column, (elems, 128))

    n2 = NVAR * NVAR
    entry = lax.broadcasted_iota(jnp.int32, (n2, NVAR * wide), 0)
    place = lax.broadcasted_iota(jnp.int32, (n2, NVAR * wide), 1)
    wanted = ((place % wide) // nb) * NVAR + place // wide
    spread_one = jnp.where(entry == wanted, 1.0, 0.0).astype(jnp.bfloat16)
    for d in range(4):
        block = lift[d].astype(jnp.bfloat16)
        lt[d] = jnp.concatenate([block] * NVAR, axis=0)
        values = jac[:, d, :]
        high = values.astype(jnp.bfloat16)
        low = (values - high.astype(jnp.float32)).astype(jnp.bfloat16)
        jx[d] = lax.dot_general(
            high, spread_one, CONTRACT_FIRST, preferred_element_type=jnp.float32
        ) + lax.dot_general(low, spread_one, CONTRACT_FIRST, preferred_element_type=jnp.float32)

    row = lax.broadcasted_iota(jnp.int32, (GROUP, unk), 0)

    def permuted(x, which, g):
        column = rel[which, rows(g)][:, 0:1]
        out = jnp.broadcast_to(x[0:1], (GROUP, unk))
        for k in range(1, BLOCK):
            out = jnp.where(column == float(k), x[k : k + 1], out)
        return out

    def couple(x, d, where):
        n = x.shape[0]
        stacked = jnp.concatenate([x[:, v * nb : (v + 1) * nb] for v in range(NVAR)], axis=0)
        spread = lax.dot_general(
            stacked.astype(jnp.bfloat16), lt[d], CONTRACT_LAST, preferred_element_type=jnp.float32
        )
        total = None
        for v in range(NVAR):
            term = jx[d, where, v * wide : v * wide + unk] * spread[v * n : (v + 1) * n]
            total = term if total is None else total + term
        return total

    def solve(resid, g, h, beside):
        flat = resid.astype(jnp.bfloat16)
        out = jnp.zeros((GROUP, unk), jnp.float32)
        for k in range(h * BLOCK, (h + 1) * BLOCK):
            product = lax.dot_general(
                flat, a_vm[g * GROUP + k], CONTRACT_LAST, preferred_element_type=jnp.float32
            )
            out = jnp.where(row == k, product, out)
            if k == h * BLOCK:
                other = beside()
        return jnp.where(row + g * GROUP < count, out, 0.0), other

    @pl.when(has_left)
    def _():
        halo_copy(oldp, 0, 0, right_dev).wait_recv()

    @pl.when(has_right)
    def _():
        halo_copy(oldp, 1, 1, left_dev).wait_recv()

    oldp[pl.ds(0, GROUP)] = halo[0]
    oldp[pl.ds(elems + GROUP, GROUP)] = halo[1]

    whole = pl.ds(0, elems)
    fix_f[...] = (
        rhs[0]
        - couple(oldp[pl.ds(GROUP - 1, elems)], 2, whole)
        - couple(oldp[pl.ds(GROUP + 1, elems)], 3, whole)
    )

    @pl.when(has_down)
    def _():
        old_copy().wait_recv()

    def arrange(g, carry):
        x = down_in[rows(g)]
        oldp[rows(g)] = jnp.where(row < BLOCK, permuted(x[:BLOCK], 1, g), permuted(x[BLOCK:], 1, g))
        return carry

    @pl.when(has_up)
    def _():
        old_copy().wait_send()

    @pl.when(has_right)
    def _():
        halo_copy(oldp, 0, 0, right_dev).wait_send()

    @pl.when(has_left)
    def _():
        halo_copy(oldp, 1, 1, left_dev).wait_send()

    lax.fori_loop(0, groups, arrange, 0)
    fix_f[...] = fix_f[...] - couple(oldp[pl.ds(0, elems)], 1, whole)

    def forward_coupling(j, g):
        return couple(permuted(fwd_in[j], 0, g), 0, rows(g))

    def backward_coupling(j, g):
        return couple(permuted(bwd_in[j], 1, g), 1, rows(g))

    def forward(g, coupled):
        a_copy(g).wait()
        fixed = fix_f[rows(g)]
        coupling = jnp.zeros((GROUP, unk), jnp.float32)
        result = jnp.zeros((GROUP, unk), jnp.float32)
        for h in range(halves):
            j = g * halves + h
            last = h == halves - 1
            g_next = jnp.minimum(g + 1, groups - 1) if last else g
            j_next = g_next * halves if last else j + 1

            @pl.when(jnp.logical_and(has_up, g < groups - 1) if last else has_up)
            def _():
                fwd_copy(j_next).wait_recv()

            solved, coupled_next = solve(
                fixed - coupled, g, h, functools.partial(forward_coupling, j_next, g_next)
            )
            fwd_snd[j] = solved[h * BLOCK : (h + 1) * BLOCK]

            @pl.when(has_down)
            def _():
                fwd_copy(j).start()

            coupling = jnp.where(row // BLOCK == h, coupled, coupling)
            result = result + solved
            coupled = coupled_next
        fix_b[rows(g)] = rhs[0, rows(g)] - coupling
        halfp[padded_rows(g)] = result
        half_out[0, rows(g)] = result

        @pl.when(jnp.logical_and(g == 0, has_left))
        def _():
            halo_copy(halfp, 1, 3, left_dev).start()

        return coupled

    @pl.when(has_up)
    def _():
        fwd_copy(0).wait_recv()

    lax.fori_loop(0, groups, forward, forward_coupling(0, 0))

    @pl.when(has_right)
    def _():
        halo_copy(halfp, 0, 2, right_dev).start()
        halo_copy(halfp, 1, 3, left_dev).wait_recv()

    halfp[pl.ds(elems + GROUP, GROUP)] = halo[3]
    later = pl.ds(GROUP, elems - GROUP)
    fix_b[later] = (
        fix_b[later]
        - couple(halfp[pl.ds(2 * GROUP - 1, elems - GROUP)], 2, later)
        - couple(halfp[pl.ds(2 * GROUP + 1, elems - GROUP)], 3, later)
    )

    def backward(i, coupled):
        g = groups - 1 - i

        @pl.when(g == 0)
        def _():
            @pl.when(has_left)
            def _():
                halo_copy(halfp, 0, 2, right_dev).wait_recv()

            halfp[pl.ds(0, GROUP)] = halo[2]
            first = pl.ds(0, GROUP)
            fix_b[first] = (
                fix_b[first]
                - couple(halfp[pl.ds(GROUP - 1, GROUP)], 2, first)
                - couple(halfp[pl.ds(GROUP + 1, GROUP)], 3, first)
            )

        fixed = fix_b[rows(g)]
        result = jnp.zeros((GROUP, unk), jnp.float32)
        for h in reversed(range(halves)):
            j = g * halves + h
            last = h == 0
            g_next = jnp.maximum(g - 1, 0) if last else g
            j_next = g_next * halves + (halves - 1 if last else h - 1)

            @pl.when(jnp.logical_and(has_down, g > 0) if last else has_down)
            def _():
                bwd_copy(j_next).wait_recv()

            solved, coupled_next = solve(
                fixed - coupled, g, h, functools.partial(backward_coupling, j_next, g_next)
            )
            bwd_snd[j] = solved[h * BLOCK : (h + 1) * BLOCK]

            @pl.when(has_up)
            def _():
                bwd_copy(j).start()

            result = result + solved
            coupled = coupled_next
        full_out[0, rows(g)] = result
        return coupled

    @pl.when(has_down)
    def _():
        bwd_copy(groups * halves - 1).wait_recv()

    lax.fori_loop(0, groups, backward, backward_coupling(groups * halves - 1, groups - 1))

    def drain(g, carry):
        @pl.when(has_down)
        def _():
            fwd_copy(g).wait_send()

        @pl.when(has_up)
        def _():
            bwd_copy(g).wait_send()

        return carry

    lax.fori_loop(0, groups * halves, drain, 0)

    @pl.when(has_right)
    def _():
        halo_copy(halfp, 0, 2, right_dev).wait_send()

    @pl.when(has_left)
    def _():
        halo_copy(halfp, 1, 3, left_dev).wait_send()


def per_device(
    right_side, old_state, block_inverse, flux_jacobian, face_lift, upstream, downstream, live_counts
):
    layers, elems, unk = right_side.shape
    assert layers == 1 and elems % GROUP == 0
    nf, nc = lax.axis_size("flow"), lax.axis_size("cross")
    nb = unk // NVAR
    wide = -(-unk // 128) * 128
    groups = elems // GROUP
    vmem = pl.BlockSpec(memory_space=pltpu.VMEM)
    hbm = pl.BlockSpec(memory_space=pltpu.HBM)
    blocks = elems // BLOCK
    jacobian = jnp.transpose(flux_jacobian[0], (2, 1, 0))
    f32 = jnp.float32
    dma = pltpu.SemaphoreType.DMA
    return pl.pallas_call(
        functools.partial(sweep_kernel, nf, nc),
        out_shape=(jax.ShapeDtypeStruct(right_side.shape, f32),) * 2,
        in_specs=[
            hbm, hbm, hbm, hbm, hbm, hbm, hbm, hbm,
        ],
        out_specs=(vmem, vmem),
        scratch_shapes=[
            pltpu.VMEM(right_side.shape, f32),
            pltpu.VMEM(old_state.shape, f32),
            pltpu.VMEM(jacobian.shape, f32),
            pltpu.VMEM(face_lift.shape, f32),
            pltpu.VMEM(upstream.shape, jnp.int32),
            pltpu.VMEM(downstream.shape, jnp.int32),
            pltpu.VMEM(live_counts.shape, jnp.int32),
            pltpu.VMEM((elems, unk, unk), jnp.bfloat16),
            pltpu.VMEM((4, elems, NVAR * wide), f32),
            pltpu.VMEM((4, unk, nb), jnp.bfloat16),
            pltpu.VMEM((elems + 2 * GROUP, unk), f32),
            pltpu.VMEM((elems + 2 * GROUP, unk), f32),
            pltpu.VMEM((elems, unk), f32),
            pltpu.VMEM((4, GROUP, unk), f32),
            pltpu.VMEM((blocks, BLOCK, unk), f32),
            pltpu.VMEM((blocks, BLOCK, unk), f32),
            pltpu.VMEM((blocks, BLOCK, unk), f32),
            pltpu.VMEM((blocks, BLOCK, unk), f32),
            pltpu.VMEM((elems, unk), f32),
            pltpu.VMEM((elems, unk), f32),
            pltpu.VMEM((2, elems, 128), f32),
            dma((7,)), dma((groups,)), dma, dma, dma((4,)), dma((4,)),
            dma((blocks,)), dma((blocks,)), dma((blocks,)), dma((blocks,)),
        ],
        compiler_params=pltpu.CompilerParams(
            collective_id=0, has_side_effects=True, vmem_limit_bytes=VMEM_BYTES
        ),
        cost_estimate=pl.CostEstimate(
            flops=4 * elems * unk * unk, bytes_accessed=2 * elems * unk * unk, transcendentals=0
        ),
        name="sweep",
    )(right_side, old_state, block_inverse, jacobian, face_lift, upstream, downstream, live_counts)


def solution(mesh):
    in_specs = (
        P("flow", "cross", None),
        P("flow", "cross", None),
        P("flow", "cross", None, None),
        P("flow", "cross", None, None),
        P(),
        P("flow", "cross"),
        P("flow", "cross"),
        P("flow", "cross"),
    )
    out_specs = (P("flow", "cross", None), P("flow", "cross", None))
    return jax.shard_map(
        per_device, mesh=mesh, in_specs=in_specs, out_specs=out_specs, check_vma=False
    )
```

```python
import functools

import jax
import jax.numpy as jnp
from jax import lax
from jax.experimental import pallas as pl
from jax.experimental.pallas import tpu as pltpu
from jax.sharding import PartitionSpec as P

NVAR = 5
GROUP = 8
BLOCK = 4
VMEM_BYTES = 64 * 1024 * 1024
MESH = pl.DeviceIdType.MESH
CONTRACT_LAST = (((1,), (1,)), ((), ()))
CONTRACT_FIRST = (((0,), (0,)), ((), ()))


def sweep_kernel(
    nf, nc,
    rhs_hbm, old_hbm, ainv, jac_hbm, lift_hbm, up_hbm, down_hbm, cnt_hbm,
    half_out, full_out,
    rhs, old, jac, lift, up, down, cnt,
    a_vm, jx, lt, oldp, result, down_in, halo, inbox, outbox, fix, rel,
    in_sem, a_sem, old_send, old_recv, halo_send, halo_recv, box_send, box_recv,
):
    elems, unk = rhs.shape[1], rhs.shape[2]
    halves = GROUP // BLOCK
    nb = unk // NVAR
    wide = -(-unk // 128) * 128
    groups = elems // GROUP
    blocks = elems // BLOCK
    halfp = result.at[0]
    f = lax.axis_index("flow")
    c = lax.axis_index("cross")
    has_up, has_down = f > 0, f < nf - 1
    has_left, has_right = c > 0, c < nc - 1
    up_dev, down_dev = {"flow": f - 1}, {"flow": f + 1}
    left_dev, right_dev = {"cross": c - 1}, {"cross": c + 1}
    neighbours = ((has_up, up_dev), (has_down, down_dev), (has_left, left_dev), (has_right, right_dev))

    def rows(g):
        return pl.ds(pl.multiple_of(g * GROUP, GROUP), GROUP)

    def padded_rows(g):
        return pl.ds(pl.multiple_of(g * GROUP + GROUP, GROUP), GROUP)

    def a_copy(g):
        return pltpu.make_async_copy(ainv.at[0, rows(g)], a_vm.at[rows(g)], a_sem.at[g])

    def remote(src, dst, ssem, rsem, dev):
        return pltpu.make_async_remote_copy(
            src_ref=src, dst_ref=dst, send_sem=ssem, recv_sem=rsem,
            device_id=dev, device_id_type=MESH,
        )

    def old_copy():
        return remote(oldp.at[pl.ds(GROUP, elems)], down_in, old_send, old_recv, up_dev)

    def halo_copy(buf, which, slot, dev):
        start = elems if which == 0 else GROUP
        return remote(buf.at[pl.ds(start, GROUP)], halo.at[slot], halo_send.at[slot], halo_recv.at[slot], dev)

    def box_copy(slot, dev):
        return remote(outbox.at[slot], inbox.at[slot], box_send.at[slot], box_recv.at[slot], dev)

    sources = (old_hbm, cnt_hbm, jac_hbm, lift_hbm, up_hbm, down_hbm, rhs_hbm)
    fetches = [
        pltpu.make_async_copy(src, dst, in_sem.at[i])
        for i, (src, dst) in enumerate(zip(sources, (old, cnt, jac, lift, up, down, rhs)))
    ]
    for fetch in fetches:
        fetch.start()
    for g in range(groups):
        a_copy(g).start()

    barrier = pltpu.get_barrier_semaphore()
    for there, dev in neighbours:
        @pl.when(there)
        def _(dev=dev):
            pl.semaphore_signal(barrier, inc=1, device_id=dev, device_id_type=MESH)

    fetches[0].wait()
    fetches[1].wait()
    count = cnt[...]
    slot = lax.broadcasted_iota(jnp.int32, (elems, unk), 0)
    oldp[pl.ds(GROUP, elems)] = jnp.where(slot < count, old[0], 0.0)

    pl.semaphore_wait(barrier, sum(there.astype(jnp.int32) for there, _ in neighbours))

    @pl.when(has_up)
    def _():
        old_copy().start()

    @pl.when(has_right)
    def _():
        halo_copy(oldp, 0, 0, right_dev).start()

    @pl.when(has_left)
    def _():
        halo_copy(oldp, 1, 1, left_dev).start()

    edge = jnp.zeros((GROUP, unk), jnp.float32)

    @pl.when(jnp.logical_not(has_up))
    def _():
        inbox[pl.ds(0, blocks)] = jnp.zeros((blocks, BLOCK, unk), jnp.float32)

    @pl.when(jnp.logical_not(has_down))
    def _():
        down_in[...] = jnp.zeros_like(down_in)
        inbox[pl.ds(blocks, blocks)] = jnp.zeros((blocks, BLOCK, unk), jnp.float32)

    @pl.when(jnp.logical_not(has_left))
    def _():
        halo[0] = edge
        halo[2] = edge

    @pl.when(jnp.logical_not(has_right))
    def _():
        halo[1] = edge
        halo[3] = edge

    for fetch in fetches[2:]:
        fetch.wait()

    square = (elems, elems)
    diagonal = lax.broadcasted_iota(jnp.int32, square, 0) == lax.broadcasted_iota(jnp.int32, square, 1)
    for i, index in enumerate((up, down)):
        local = (index[...] % BLOCK).astype(jnp.float32)
        column = jnp.sum(jnp.where(diagonal, jnp.broadcast_to(local, square), 0.0), axis=1, keepdims=True)
        rel[i] = jnp.broadcast_to(column, (elems, 128))

    n2 = NVAR * NVAR
    entry = lax.broadcasted_iota(jnp.int32, (n2, NVAR * wide), 0)
    place = lax.broadcasted_iota(jnp.int32, (n2, NVAR * wide), 1)
    wanted = ((place % wide) // nb) * NVAR + place // wide
    spread_one = jnp.where(entry == wanted, 1.0, 0.0).astype(jnp.bfloat16)
    for d in range(4):
        block = lift[d].astype(jnp.bfloat16)
        lt[d] = jnp.concatenate([block] * NVAR, axis=0)
        values = jac[:, d, :]
        high = values.astype(jnp.bfloat16)
        low = (values - high.astype(jnp.float32)).astype(jnp.bfloat16)
        jx[d] = lax.dot_general(
            high, spread_one, CONTRACT_FIRST, preferred_element_type=jnp.float32
        ) + lax.dot_general(low, spread_one, CONTRACT_FIRST, preferred_element_type=jnp.float32)

    row = lax.broadcasted_iota(jnp.int32, (GROUP, unk), 0)

    def permuted(x, which, g):
        column = rel[which, rows(g)][:, 0:1]
        out = jnp.broadcast_to(x[0:1], (GROUP, unk))
        for k in range(1, BLOCK):
            out = jnp.where(column == float(k), x[k : k + 1], out)
        return out

    def couple(x, d, where):
        n = x.shape[0]
        stacked = jnp.concatenate([x[:, v * nb : (v + 1) * nb] for v in range(NVAR)], axis=0)
        spread = lax.dot_general(
            stacked.astype(jnp.bfloat16), lt[d], CONTRACT_LAST, preferred_element_type=jnp.float32
        )
        total = None
        for v in range(NVAR):
            term = jx[d, where, v * wide : v * wide + unk] * spread[v * n : (v + 1) * n]
            total = term if total is None else total + term
        return total

    def solve(resid, j):
        flat = resid.astype(jnp.bfloat16)
        first = (j % halves) * BLOCK
        out = jnp.zeros((GROUP, unk), jnp.float32)
        for k in range(BLOCK):
            product = lax.dot_general(
                flat, a_vm[j * BLOCK + k], CONTRACT_LAST, preferred_element_type=jnp.float32
            )
            out = jnp.where(row == first + k, product, out)
        return jnp.where(row + (j // halves) * GROUP < count, out, 0.0)

    def prepare_forward():
        @pl.when(has_left)
        def _():
            halo_copy(oldp, 0, 0, right_dev).wait_recv()

        @pl.when(has_right)
        def _():
            halo_copy(oldp, 1, 1, left_dev).wait_recv()

        oldp[pl.ds(0, GROUP)] = halo[0]
        oldp[pl.ds(elems + GROUP, GROUP)] = halo[1]

        whole = pl.ds(0, elems)
        sides = couple(oldp[pl.ds(GROUP - 1, elems)], 2, whole) + couple(
            oldp[pl.ds(GROUP + 1, elems)], 3, whole
        )

        @pl.when(has_down)
        def _():
            old_copy().wait_recv()

        @pl.when(has_up)
        def _():
            old_copy().wait_send()

        @pl.when(has_right)
        def _():
            halo_copy(oldp, 0, 0, right_dev).wait_send()

        @pl.when(has_left)
        def _():
            halo_copy(oldp, 1, 1, left_dev).wait_send()

        for g in range(groups):
            x = down_in[pl.ds(g * GROUP, GROUP)]
            oldp[pl.ds(g * GROUP, GROUP)] = jnp.where(
                row < BLOCK, permuted(x[:BLOCK], 1, g), permuted(x[BLOCK:], 1, g)
            )
        fix[0] = rhs[0] - sides - couple(oldp[pl.ds(0, elems)], 1, whole)

    def prepare_backward():
        @pl.when(has_right)
        def _():
            halo_copy(halfp, 0, 2, right_dev).start()
            halo_copy(halfp, 1, 3, left_dev).wait_recv()

        halfp[pl.ds(elems + GROUP, GROUP)] = halo[3]
        later = pl.ds(GROUP, elems - GROUP)
        fix[1, later] = (
            fix[1, later]
            - couple(halfp[pl.ds(2 * GROUP - 1, elems - GROUP)], 2, later)
            - couple(halfp[pl.ds(2 * GROUP + 1, elems - GROUP)], 3, later)
        )

    def prepare_first_group():
        @pl.when(has_left)
        def _():
            halo_copy(halfp, 0, 2, right_dev).wait_recv()

        halfp[pl.ds(0, GROUP)] = halo[2]
        first = pl.ds(0, GROUP)
        fix[1, first] = (
            fix[1, first]
            - couple(halfp[pl.ds(GROUP - 1, GROUP)], 2, first)
            - couple(halfp[pl.ds(GROUP + 1, GROUP)], 3, first)
        )

    def step(t, carry):
        done = jnp.maximum(t - 1, 0)
        phase = done // blocks
        u = done % blocks
        j = phase * (blocks - 1) + (1 - 2 * phase) * u
        g = j // halves
        slot = phase * blocks + j + (1 - jnp.minimum(t, 1)) * (2 * blocks)
        forward = jnp.logical_and(t > 0, phase == 0)
        backward = phase == 1

        @pl.when(t == 1)
        def _():
            prepare_forward()

        @pl.when(t == blocks + 1)
        def _():
            prepare_backward()

        @pl.when(t == 2 * blocks + 1 - halves)
        def _():
            prepare_first_group()

        @pl.when(jnp.logical_or(t == 0, jnp.logical_and(jnp.logical_and(forward, t > 1), u % halves == 0)))
        def _():
            a_copy(g).wait()

        @pl.when(jnp.logical_or(jnp.logical_and(forward, has_up), jnp.logical_and(backward, has_down)))
        def _():
            box_copy(slot, up_dev).wait_recv()

        coupled = couple(permuted(inbox[slot], phase, g), phase, rows(g))
        solved = solve(fix[phase, rows(g)] - coupled, j)
        half = j % halves
        outbox[slot] = jnp.where(half == 0, solved[:BLOCK], solved[BLOCK:])

        @pl.when(jnp.logical_and(forward, has_down))
        def _():
            box_copy(slot, down_dev).start()

        @pl.when(jnp.logical_and(backward, has_up))
        def _():
            box_copy(slot, up_dev).start()

        fresh = u % halves == 0
        result[phase, padded_rows(g)] = jnp.where(fresh, 0.0, result[phase, padded_rows(g)]) + solved

        @pl.when(phase == 0)
        def _():
            base = jnp.where(fresh, rhs[0, rows(g)], fix[1, rows(g)])
            fix[1, rows(g)] = base - jnp.where(row // BLOCK == half, coupled, 0.0)

        @pl.when(jnp.logical_and(t == halves, has_left))
        def _():
            halo_copy(halfp, 1, 3, left_dev).start()

        return carry

    lax.fori_loop(0, 2 * blocks + 1, step, 0)
    half_out[0] = result[0, pl.ds(GROUP, elems)]
    full_out[0] = result[1, pl.ds(GROUP, elems)]

    def drain(j, carry):
        @pl.when(has_down)
        def _():
            box_copy(j, down_dev).wait_send()

        @pl.when(has_up)
        def _():
            box_copy(blocks + j, up_dev).wait_send()

        return carry

    lax.fori_loop(0, blocks, drain, 0)

    @pl.when(has_right)
    def _():
        halo_copy(halfp, 0, 2, right_dev).wait_send()

    @pl.when(has_left)
    def _():
        halo_copy(halfp, 1, 3, left_dev).wait_send()


def per_device(
    right_side, old_state, block_inverse, flux_jacobian, face_lift, upstream, downstream, live_counts
):
    layers, elems, unk = right_side.shape
    assert layers == 1 and elems % GROUP == 0
    nf, nc = lax.axis_size("flow"), lax.axis_size("cross")
    nb = unk // NVAR
    wide = -(-unk // 128) * 128
    groups = elems // GROUP
    vmem = pl.BlockSpec(memory_space=pltpu.VMEM)
    hbm = pl.BlockSpec(memory_space=pltpu.HBM)
    blocks = elems // BLOCK
    jacobian = jnp.transpose(flux_jacobian[0], (2, 1, 0))
    f32 = jnp.float32
    dma = pltpu.SemaphoreType.DMA
    return pl.pallas_call(
        functools.partial(sweep_kernel, nf, nc),
        out_shape=(jax.ShapeDtypeStruct(right_side.shape, f32),) * 2,
        in_specs=[
            hbm, hbm, hbm, hbm, hbm, hbm, hbm, hbm,
        ],
        out_specs=(vmem, vmem),
        scratch_shapes=[
            pltpu.VMEM(right_side.shape, f32),
            pltpu.VMEM(old_state.shape, f32),
            pltpu.VMEM(jacobian.shape, f32),
            pltpu.VMEM(face_lift.shape, f32),
            pltpu.VMEM(upstream.shape, jnp.int32),
            pltpu.VMEM(downstream.shape, jnp.int32),
            pltpu.VMEM(live_counts.shape, jnp.int32),
            pltpu.VMEM((elems, unk, unk), jnp.bfloat16),
            pltpu.VMEM((4, elems, NVAR * wide), f32),
            pltpu.VMEM((4, unk, nb), jnp.bfloat16),
            pltpu.VMEM((elems + 2 * GROUP, unk), f32),
            pltpu.VMEM((2, elems + 2 * GROUP, unk), f32),
            pltpu.VMEM((elems, unk), f32),
            pltpu.VMEM((4, GROUP, unk), f32),
            pltpu.VMEM((2 * blocks + 1, BLOCK, unk), f32),
            pltpu.VMEM((2 * blocks + 1, BLOCK, unk), f32),
            pltpu.VMEM((2, elems, unk), f32),
            pltpu.VMEM((2, elems, 128), f32),
            dma((7,)), dma((groups,)), dma, dma, dma((4,)), dma((4,)),
            dma((2 * blocks,)), dma((2 * blocks,)),
        ],
        compiler_params=pltpu.CompilerParams(
            collective_id=0, has_side_effects=True, vmem_limit_bytes=VMEM_BYTES
        ),
        cost_estimate=pl.CostEstimate(
            flops=4 * elems * unk * unk, bytes_accessed=2 * elems * unk * unk, transcendentals=0
        ),
        name="sweep",
    )(right_side, old_state, block_inverse, jacobian, face_lift, upstream, downstream, live_counts)


def solution(mesh):
    in_specs = (
        P("flow", "cross", None),
        P("flow", "cross", None),
        P("flow", "cross", None, None),
        P("flow", "cross", None, None),
        P(),
        P("flow", "cross"),
        P("flow", "cross"),
        P("flow", "cross"),
    )
    out_specs = (P("flow", "cross", None), P("flow", "cross", None))
    return jax.shard_map(
        per_device, mesh=mesh, in_specs=in_specs, out_specs=out_specs, check_vma=False
    )
```

```python
import functools

import jax
import jax.numpy as jnp
from jax import lax
from jax.experimental import pallas as pl
from jax.experimental.pallas import tpu as pltpu
from jax.sharding import PartitionSpec as P

NVAR = 5
GROUP = 8
BLOCK = 4
VMEM_BYTES = 64 * 1024 * 1024
MESH = pl.DeviceIdType.MESH
CONTRACT_LAST = (((1,), (1,)), ((), ()))
CONTRACT_FIRST = (((0,), (0,)), ((), ()))


def sweep_kernel(
    nf, nc,
    rhs_hbm, old_hbm, ainv, jac_hbm, lift_hbm, up_hbm, down_hbm, cnt_hbm,
    half_out, full_out,
    rhs, old, jac, lift, up, down, cnt,
    a_vm, jx, lt, oldp, result, down_in, halo, inbox, outbox, fix, rel, packed, ahead,
    in_sem, a_sem, old_send, old_recv, halo_send, halo_recv, box_send, box_recv,
):
    elems, unk = rhs.shape[1], rhs.shape[2]
    halves = GROUP // BLOCK
    nb = unk // NVAR
    wide = -(-unk // 128) * 128
    groups = elems // GROUP
    blocks = elems // BLOCK
    halfp = result.at[0]
    main = unk - unk // NVAR
    rest = unk - main
    f = lax.axis_index("flow")
    c = lax.axis_index("cross")
    has_up, has_down = f > 0, f < nf - 1
    has_left, has_right = c > 0, c < nc - 1
    up_dev, down_dev = {"flow": f - 1}, {"flow": f + 1}
    left_dev, right_dev = {"cross": c - 1}, {"cross": c + 1}
    neighbours = ((has_up, up_dev), (has_down, down_dev), (has_left, left_dev), (has_right, right_dev))

    def rows(g):
        return pl.ds(pl.multiple_of(g * GROUP, GROUP), GROUP)

    def padded_rows(g):
        return pl.ds(pl.multiple_of(g * GROUP + GROUP, GROUP), GROUP)

    def a_copy(g):
        return pltpu.make_async_copy(ainv.at[0, rows(g)], a_vm.at[rows(g)], a_sem.at[g])

    def remote(src, dst, ssem, rsem, dev):
        return pltpu.make_async_remote_copy(
            src_ref=src, dst_ref=dst, send_sem=ssem, recv_sem=rsem,
            device_id=dev, device_id_type=MESH,
        )

    def old_copy():
        return remote(oldp.at[pl.ds(GROUP, elems)], down_in, old_send, old_recv, up_dev)

    def halo_copy(buf, which, slot, dev):
        start = elems if which == 0 else GROUP
        return remote(buf.at[pl.ds(start, GROUP)], halo.at[slot], halo_send.at[slot], halo_recv.at[slot], dev)

    def box_copy(slot, dev):
        return remote(outbox.at[slot], inbox.at[slot], box_send.at[slot], box_recv.at[slot], dev)

    sources = (old_hbm, cnt_hbm, jac_hbm, lift_hbm, up_hbm, down_hbm, rhs_hbm)
    fetches = [
        pltpu.make_async_copy(src, dst, in_sem.at[i])
        for i, (src, dst) in enumerate(zip(sources, (old, cnt, jac, lift, up, down, rhs)))
    ]
    for fetch in fetches:
        fetch.start()
    for g in range(groups):
        a_copy(g).start()

    barrier = pltpu.get_barrier_semaphore()
    for there, dev in neighbours:
        @pl.when(there)
        def _(dev=dev):
            pl.semaphore_signal(barrier, inc=1, device_id=dev, device_id_type=MESH)

    fetches[0].wait()
    fetches[1].wait()
    count = cnt[...]
    slot = lax.broadcasted_iota(jnp.int32, (elems, unk), 0)
    oldp[pl.ds(GROUP, elems)] = jnp.where(slot < count, old[0], 0.0)

    pl.semaphore_wait(barrier, sum(there.astype(jnp.int32) for there, _ in neighbours))

    @pl.when(has_up)
    def _():
        old_copy().start()

    @pl.when(has_right)
    def _():
        halo_copy(oldp, 0, 0, right_dev).start()

    @pl.when(has_left)
    def _():
        halo_copy(oldp, 1, 1, left_dev).start()

    edge = jnp.zeros((GROUP, unk), jnp.float32)

    @pl.when(jnp.logical_not(has_up))
    def _():
        inbox[pl.ds(0, blocks)] = jnp.zeros((blocks, BLOCK, unk), jnp.float32)

    @pl.when(jnp.logical_not(has_down))
    def _():
        down_in[...] = jnp.zeros_like(down_in)
        inbox[pl.ds(blocks, blocks)] = jnp.zeros((blocks, BLOCK, unk), jnp.float32)

    @pl.when(jnp.logical_not(has_left))
    def _():
        halo[0] = edge
        halo[2] = edge

    @pl.when(jnp.logical_not(has_right))
    def _():
        halo[1] = edge
        halo[3] = edge

    for fetch in fetches[2:]:
        fetch.wait()

    square = (elems, elems)
    diagonal = lax.broadcasted_iota(jnp.int32, square, 0) == lax.broadcasted_iota(jnp.int32, square, 1)
    for i, index in enumerate((up, down)):
        local = (index[...] % BLOCK).astype(jnp.float32)
        column = jnp.sum(jnp.where(diagonal, jnp.broadcast_to(local, square), 0.0), axis=1, keepdims=True)
        rel[i] = jnp.broadcast_to(column, (elems, 128))

    n2 = NVAR * NVAR
    entry = lax.broadcasted_iota(jnp.int32, (n2, NVAR * wide), 0)
    place = lax.broadcasted_iota(jnp.int32, (n2, NVAR * wide), 1)
    wanted = ((place % wide) // nb) * NVAR + place // wide
    spread_one = jnp.where(entry == wanted, 1.0, 0.0).astype(jnp.bfloat16)
    for d in range(4):
        block = lift[d].astype(jnp.bfloat16)
        lt[d] = jnp.concatenate([block] * NVAR, axis=0)
        values = jac[:, d, :]
        high = values.astype(jnp.bfloat16)
        low = (values - high.astype(jnp.float32)).astype(jnp.bfloat16)
        jx[d] = lax.dot_general(
            high, spread_one, CONTRACT_FIRST, preferred_element_type=jnp.float32
        ) + lax.dot_general(low, spread_one, CONTRACT_FIRST, preferred_element_type=jnp.float32)

    row = lax.broadcasted_iota(jnp.int32, (GROUP, unk), 0)

    def permuted(x, which, g):
        column = rel[which, rows(g)][:, 0:1]
        out = jnp.broadcast_to(x[0:1], (GROUP, unk))
        for k in range(1, BLOCK):
            out = jnp.where(column == float(k), x[k : k + 1], out)
        return out

    def couple(x, d, where):
        n = x.shape[0]
        stacked = jnp.concatenate([x[:, v * nb : (v + 1) * nb] for v in range(NVAR)], axis=0)
        spread = lax.dot_general(
            stacked.astype(jnp.bfloat16), lt[d], CONTRACT_LAST, preferred_element_type=jnp.float32
        )
        total = None
        for v in range(NVAR):
            term = jx[d, where, v * wide : v * wide + unk] * spread[v * n : (v + 1) * n]
            total = term if total is None else total + term
        return total

    def solve(resid, j, beside):
        first = (j % halves) * BLOCK
        tail = jnp.concatenate([resid[:, main:]] * BLOCK, axis=1)
        lane = lax.broadcasted_iota(jnp.int32, (GROUP, BLOCK * rest), 1)
        line = lax.broadcasted_iota(jnp.int32, (GROUP, BLOCK * rest), 0)
        tail = jnp.where(lane // rest == line % BLOCK, tail, 0.0).astype(jnp.bfloat16)
        head = resid[:, :main].astype(jnp.bfloat16)
        out = jnp.zeros((GROUP, unk), jnp.float32)
        for k in range(BLOCK):
            product = lax.dot_general(
                head, a_vm[j * BLOCK + k, :, 0:main], CONTRACT_LAST, preferred_element_type=jnp.float32
            )
            out = jnp.where(row == first + k, product, out)
            if k == 0:
                other = beside()
        out = out + lax.dot_general(tail, packed[j], CONTRACT_LAST, preferred_element_type=jnp.float32)
        mine = jnp.logical_and(row // BLOCK == j % halves, row + (j // halves) * GROUP < count)
        return jnp.where(mine, out, 0.0), other

    def pack(j, carry):
        packed[j] = jnp.concatenate([a_vm[j * BLOCK + k, :, main:] for k in range(BLOCK)], axis=1)
        return carry

    def wait_a(g, carry):
        a_copy(g).wait()
        return carry

    lax.fori_loop(0, groups, wait_a, 0)
    lax.fori_loop(0, blocks, pack, 0)

    def prepare_forward():
        @pl.when(has_left)
        def _():
            halo_copy(oldp, 0, 0, right_dev).wait_recv()

        @pl.when(has_right)
        def _():
            halo_copy(oldp, 1, 1, left_dev).wait_recv()

        oldp[pl.ds(0, GROUP)] = halo[0]
        oldp[pl.ds(elems + GROUP, GROUP)] = halo[1]

        whole = pl.ds(0, elems)
        sides = couple(oldp[pl.ds(GROUP - 1, elems)], 2, whole) + couple(
            oldp[pl.ds(GROUP + 1, elems)], 3, whole
        )

        @pl.when(has_down)
        def _():
            old_copy().wait_recv()

        @pl.when(has_up)
        def _():
            old_copy().wait_send()

        @pl.when(has_right)
        def _():
            halo_copy(oldp, 0, 0, right_dev).wait_send()

        @pl.when(has_left)
        def _():
            halo_copy(oldp, 1, 1, left_dev).wait_send()

        for g in range(groups):
            x = down_in[pl.ds(g * GROUP, GROUP)]
            oldp[pl.ds(g * GROUP, GROUP)] = jnp.where(
                row < BLOCK, permuted(x[:BLOCK], 1, g), permuted(x[BLOCK:], 1, g)
            )
        fix[0] = rhs[0] - sides - couple(oldp[pl.ds(0, elems)], 1, whole)

    def prepare_backward():
        @pl.when(has_right)
        def _():
            halo_copy(halfp, 0, 2, right_dev).start()
            halo_copy(halfp, 1, 3, left_dev).wait_recv()

        halfp[pl.ds(elems + GROUP, GROUP)] = halo[3]
        later = pl.ds(GROUP, elems - GROUP)
        fix[1, later] = (
            fix[1, later]
            - couple(halfp[pl.ds(2 * GROUP - 1, elems - GROUP)], 2, later)
            - couple(halfp[pl.ds(2 * GROUP + 1, elems - GROUP)], 3, later)
        )

    def prepare_first_group():
        @pl.when(has_left)
        def _():
            halo_copy(halfp, 0, 2, right_dev).wait_recv()

        halfp[pl.ds(0, GROUP)] = halo[2]
        first = pl.ds(0, GROUP)
        fix[1, first] = (
            fix[1, first]
            - couple(halfp[pl.ds(GROUP - 1, GROUP)], 2, first)
            - couple(halfp[pl.ds(GROUP + 1, GROUP)], 3, first)
        )

    def coupling(slot, phase, g):
        return couple(permuted(inbox[slot], phase, g), phase, rows(g))

    def step(t, carry):
        done = jnp.maximum(t - 1, 0)
        phase = done // blocks
        u = done % blocks
        j = phase * (blocks - 1) + (1 - 2 * phase) * u
        g = j // halves
        slot = phase * blocks + j + (1 - jnp.minimum(t, 1)) * (2 * blocks)
        forward = jnp.logical_and(t > 0, phase == 0)
        backward = phase == 1

        @pl.when(t == 1)
        def _():
            prepare_forward()

        @pl.when(t == blocks + 1)
        def _():
            prepare_backward()

        @pl.when(t == 2 * blocks + 1 - halves)
        def _():
            prepare_first_group()

        inbound = jnp.logical_or(jnp.logical_and(forward, has_up), jnp.logical_and(backward, has_down))
        opening = jnp.logical_and(t > 0, u == 0)
        following = jnp.logical_and(u > 0, u < blocks - 1)
        direction = 1 - 2 * phase
        g_next = jnp.clip(j + direction, 0, blocks - 1) // halves

        @pl.when(opening)
        def _():
            @pl.when(inbound)
            def _():
                box_copy(slot, up_dev).wait_recv()

            ahead[...] = coupling(slot, phase, g)

        @pl.when(jnp.logical_and(following, inbound))
        def _():
            box_copy(slot + direction, up_dev).wait_recv()

        ok = following.astype(jnp.int32)
        slot_next = ok * (slot + direction) + (1 - ok) * (2 * blocks)
        coupled = ahead[...]
        solved, coupled_next = solve(
            fix[phase, rows(g)] - coupled, j, lambda: coupling(slot_next, phase, g_next)
        )
        half = j % halves
        outbox[slot] = jnp.where(half == 0, solved[:BLOCK], solved[BLOCK:])

        @pl.when(jnp.logical_and(forward, has_down))
        def _():
            box_copy(slot, down_dev).start()

        @pl.when(jnp.logical_and(backward, has_up))
        def _():
            box_copy(slot, up_dev).start()

        ahead[...] = coupled_next

        @pl.when(opening)
        def _():
            @pl.when(inbound)
            def _():
                box_copy(slot + direction, up_dev).wait_recv()

            ahead[...] = coupling(slot + direction, phase, g_next)

        fresh = u % halves == 0
        result[phase, padded_rows(g)] = jnp.where(fresh, 0.0, result[phase, padded_rows(g)]) + solved

        @pl.when(phase == 0)
        def _():
            base = jnp.where(fresh, rhs[0, rows(g)], fix[1, rows(g)])
            fix[1, rows(g)] = base - jnp.where(row // BLOCK == half, coupled, 0.0)

        @pl.when(jnp.logical_and(t == halves, has_left))
        def _():
            halo_copy(halfp, 1, 3, left_dev).start()

        return carry

    lax.fori_loop(0, 2 * blocks + 1, step, 0)
    half_out[0] = result[0, pl.ds(GROUP, elems)]
    full_out[0] = result[1, pl.ds(GROUP, elems)]

    def drain(j, carry):
        @pl.when(has_down)
        def _():
            box_copy(j, down_dev).wait_send()

        @pl.when(has_up)
        def _():
            box_copy(blocks + j, up_dev).wait_send()

        return carry

    lax.fori_loop(0, blocks, drain, 0)

    @pl.when(has_right)
    def _():
        halo_copy(halfp, 0, 2, right_dev).wait_send()

    @pl.when(has_left)
    def _():
        halo_copy(halfp, 1, 3, left_dev).wait_send()


def per_device(
    right_side, old_state, block_inverse, flux_jacobian, face_lift, upstream, downstream, live_counts
):
    layers, elems, unk = right_side.shape
    assert layers == 1 and elems % GROUP == 0
    nf, nc = lax.axis_size("flow"), lax.axis_size("cross")
    nb = unk // NVAR
    wide = -(-unk // 128) * 128
    groups = elems // GROUP
    vmem = pl.BlockSpec(memory_space=pltpu.VMEM)
    hbm = pl.BlockSpec(memory_space=pltpu.HBM)
    blocks = elems // BLOCK
    jacobian = jnp.transpose(flux_jacobian[0], (2, 1, 0))
    f32 = jnp.float32
    dma = pltpu.SemaphoreType.DMA
    return pl.pallas_call(
        functools.partial(sweep_kernel, nf, nc),
        out_shape=(jax.ShapeDtypeStruct(right_side.shape, f32),) * 2,
        in_specs=[
            hbm, hbm, hbm, hbm, hbm, hbm, hbm, hbm,
        ],
        out_specs=(vmem, vmem),
        scratch_shapes=[
            pltpu.VMEM(right_side.shape, f32),
            pltpu.VMEM(old_state.shape, f32),
            pltpu.VMEM(jacobian.shape, f32),
            pltpu.VMEM(face_lift.shape, f32),
            pltpu.VMEM(upstream.shape, jnp.int32),
            pltpu.VMEM(downstream.shape, jnp.int32),
            pltpu.VMEM(live_counts.shape, jnp.int32),
            pltpu.VMEM((elems, unk, unk), jnp.bfloat16),
            pltpu.VMEM((4, elems, NVAR * wide), f32),
            pltpu.VMEM((4, unk, nb), jnp.bfloat16),
            pltpu.VMEM((elems + 2 * GROUP, unk), f32),
            pltpu.VMEM((2, elems + 2 * GROUP, unk), f32),
            pltpu.VMEM((elems, unk), f32),
            pltpu.VMEM((4, GROUP, unk), f32),
            pltpu.VMEM((2 * blocks + 1, BLOCK, unk), f32),
            pltpu.VMEM((2 * blocks + 1, BLOCK, unk), f32),
            pltpu.VMEM((2, elems, unk), f32),
            pltpu.VMEM((2, elems, 128), f32),
            pltpu.VMEM((blocks, unk, BLOCK * (unk // NVAR)), jnp.bfloat16),
            pltpu.VMEM((GROUP, unk), f32),
            dma((7,)), dma((groups,)), dma, dma, dma((4,)), dma((4,)),
            dma((2 * blocks,)), dma((2 * blocks,)),
        ],
        compiler_params=pltpu.CompilerParams(
            collective_id=0, has_side_effects=True, vmem_limit_bytes=VMEM_BYTES
        ),
        cost_estimate=pl.CostEstimate(
            flops=4 * elems * unk * unk, bytes_accessed=2 * elems * unk * unk, transcendentals=0
        ),
        name="sweep",
    )(right_side, old_state, block_inverse, jacobian, face_lift, upstream, downstream, live_counts)


def solution(mesh):
    in_specs = (
        P("flow", "cross", None),
        P("flow", "cross", None),
        P("flow", "cross", None, None),
        P("flow", "cross", None, None),
        P(),
        P("flow", "cross"),
        P("flow", "cross"),
        P("flow", "cross"),
    )
    out_specs = (P("flow", "cross", None), P("flow", "cross", None))
    return jax.shard_map(
        per_device, mesh=mesh, in_specs=in_specs, out_specs=out_specs, check_vma=False
    )
```

```python
import functools

import jax
import jax.numpy as jnp
from jax import lax
from jax.experimental import pallas as pl
from jax.experimental.pallas import tpu as pltpu
from jax.sharding import PartitionSpec as P

NVAR = 5
GROUP = 8
VMEM_BYTES = 64 * 1024 * 1024
MESH = pl.DeviceIdType.MESH
CONTRACT_LAST = (((1,), (1,)), ((), ()))
CONTRACT_FIRST = (((0,), (0,)), ((), ()))


def sweep_kernel(
    nf, nc,
    rhs_hbm, old_hbm, ainv, jac_hbm, lift_hbm, up_hbm, down_hbm, cnt_hbm,
    half_hbm, full_hbm,
    rhs, old, jac, lift, up, down, cnt,
    a_vm, jx, lt, oldp, result, down_in, halo, inbox, outbox, fix, rel, coupled_ref,
    in_sem, out_sem, a_sem, old_send, old_recv, halo_send, halo_recv, box_send, box_recv,
):
    elems, unk = rhs.shape[1], rhs.shape[2]
    nb = unk // NVAR
    wide = -(-unk // 128) * 128
    groups = elems // GROUP
    blocks = elems // GROUP
    halfp = result.at[0]
    f = lax.axis_index("flow")
    c = lax.axis_index("cross")
    has_up, has_down = f > 0, f < nf - 1
    has_left, has_right = c > 0, c < nc - 1
    up_dev, down_dev = {"flow": f - 1}, {"flow": f + 1}
    left_dev, right_dev = {"cross": c - 1}, {"cross": c + 1}
    neighbours = ((has_up, up_dev), (has_down, down_dev), (has_left, left_dev), (has_right, right_dev))

    def rows(g):
        return pl.ds(pl.multiple_of(g * GROUP, GROUP), GROUP)

    def padded_rows(g):
        return pl.ds(pl.multiple_of(g * GROUP + GROUP, GROUP), GROUP)

    def a_copy(g):
        return pltpu.make_async_copy(ainv.at[0, rows(g)], a_vm.at[rows(g)], a_sem.at[g])

    def remote(src, dst, ssem, rsem, dev):
        return pltpu.make_async_remote_copy(
            src_ref=src, dst_ref=dst, send_sem=ssem, recv_sem=rsem,
            device_id=dev, device_id_type=MESH,
        )

    def old_copy():
        return remote(oldp.at[pl.ds(GROUP, elems)], down_in, old_send, old_recv, up_dev)

    def halo_copy(buf, which, slot, dev):
        start = elems if which == 0 else GROUP
        return remote(buf.at[pl.ds(start, GROUP)], halo.at[slot], halo_send.at[slot], halo_recv.at[slot], dev)

    def box_copy(slot, dev):
        return remote(outbox.at[slot], inbox.at[slot], box_send.at[slot], box_recv.at[slot], dev)

    sources = (old_hbm, cnt_hbm, jac_hbm, lift_hbm, up_hbm, down_hbm, rhs_hbm)
    fetches = [
        pltpu.make_async_copy(src, dst, in_sem.at[i])
        for i, (src, dst) in enumerate(zip(sources, (old, cnt, jac, lift, up, down, rhs)))
    ]
    for fetch in fetches:
        fetch.start()
    for g in range(groups):
        a_copy(g).start()

    barrier = pltpu.get_barrier_semaphore()
    for there, dev in neighbours:
        @pl.when(there)
        def _(dev=dev):
            pl.semaphore_signal(barrier, inc=1, device_id=dev, device_id_type=MESH)

    fetches[0].wait()
    fetches[1].wait()
    count = cnt[...]
    slot = lax.broadcasted_iota(jnp.int32, (elems, unk), 0)
    oldp[pl.ds(GROUP, elems)] = jnp.where(slot < count, old[0], 0.0)

    pl.semaphore_wait(barrier, sum(there.astype(jnp.int32) for there, _ in neighbours))

    @pl.when(has_up)
    def _():
        old_copy().start()

    @pl.when(has_right)
    def _():
        halo_copy(oldp, 0, 0, right_dev).start()

    @pl.when(has_left)
    def _():
        halo_copy(oldp, 1, 1, left_dev).start()

    edge = jnp.zeros((GROUP, unk), jnp.float32)

    @pl.when(jnp.logical_not(has_up))
    def _():
        coupled_ref[...] = edge

    @pl.when(jnp.logical_not(has_down))
    def _():
        down_in[...] = jnp.zeros_like(down_in)

    @pl.when(jnp.logical_not(has_left))
    def _():
        halo[0] = edge
        halo[2] = edge

    @pl.when(jnp.logical_not(has_right))
    def _():
        halo[1] = edge
        halo[3] = edge

    for fetch in fetches[2:]:
        fetch.wait()

    square = (elems, elems)
    diagonal = lax.broadcasted_iota(jnp.int32, square, 0) == lax.broadcasted_iota(jnp.int32, square, 1)
    for i, index in enumerate((up, down)):
        local = (index[...] % GROUP).astype(jnp.float32)
        column = jnp.sum(jnp.where(diagonal, jnp.broadcast_to(local, square), 0.0), axis=1, keepdims=True)
        rel[i] = jnp.broadcast_to(column, (elems, 128))

    n2 = NVAR * NVAR
    entry = lax.broadcasted_iota(jnp.int32, (n2, NVAR * wide), 0)
    place = lax.broadcasted_iota(jnp.int32, (n2, NVAR * wide), 1)
    wanted = ((place % wide) // nb) * NVAR + place // wide
    spread_one = jnp.where(entry == wanted, 1.0, 0.0).astype(jnp.bfloat16)
    for d in range(4):
        block = lift[d].astype(jnp.bfloat16)
        lt[d] = jnp.concatenate([block] * NVAR, axis=0)
        values = jac[:, d, :]
        high = values.astype(jnp.bfloat16)
        low = (values - high.astype(jnp.float32)).astype(jnp.bfloat16)
        jx[d] = lax.dot_general(
            high, spread_one, CONTRACT_FIRST, preferred_element_type=jnp.float32
        ) + lax.dot_general(low, spread_one, CONTRACT_FIRST, preferred_element_type=jnp.float32)

    row = lax.broadcasted_iota(jnp.int32, (GROUP, unk), 0)

    def permuted(x, which, g):
        column = rel[which, rows(g)][:, 0:1]
        out = jnp.broadcast_to(x[0:1], (GROUP, unk))
        for k in range(1, GROUP):
            out = jnp.where(column == float(k), x[k : k + 1], out)
        return out

    def couple(x, d, where):
        n = x.shape[0]
        stacked = jnp.concatenate([x[:, v * nb : (v + 1) * nb] for v in range(NVAR)], axis=0)
        spread = lax.dot_general(
            stacked.astype(jnp.bfloat16), lt[d], CONTRACT_LAST, preferred_element_type=jnp.float32
        )
        total = None
        for v in range(NVAR):
            term = jx[d, where, v * wide : v * wide + unk] * spread[v * n : (v + 1) * n]
            total = term if total is None else total + term
        return total

    def solve(resid, j):
        flat = resid.astype(jnp.bfloat16)
        out = jnp.zeros((GROUP, unk), jnp.float32)
        for k in range(GROUP):
            product = lax.dot_general(
                flat, a_vm[j * GROUP + k], CONTRACT_LAST, preferred_element_type=jnp.float32
            )
            out = jnp.where(row == k, product, out)
        return jnp.where(row + j * GROUP < count, out, 0.0)

    def prepare_forward():
        @pl.when(has_left)
        def _():
            halo_copy(oldp, 0, 0, right_dev).wait_recv()

        @pl.when(has_right)
        def _():
            halo_copy(oldp, 1, 1, left_dev).wait_recv()

        oldp[pl.ds(0, GROUP)] = halo[0]
        oldp[pl.ds(elems + GROUP, GROUP)] = halo[1]

        whole = pl.ds(0, elems)
        sides = couple(oldp[pl.ds(GROUP - 1, elems)], 2, whole) + couple(
            oldp[pl.ds(GROUP + 1, elems)], 3, whole
        )

        @pl.when(has_down)
        def _():
            old_copy().wait_recv()

        @pl.when(has_up)
        def _():
            old_copy().wait_send()

        @pl.when(has_right)
        def _():
            halo_copy(oldp, 0, 0, right_dev).wait_send()

        @pl.when(has_left)
        def _():
            halo_copy(oldp, 1, 1, left_dev).wait_send()

        for g in range(groups):
            x = down_in[pl.ds(g * GROUP, GROUP)]
            oldp[pl.ds(g * GROUP, GROUP)] = permuted(x, 1, g)
        fix[0] = rhs[0] - sides - couple(oldp[pl.ds(0, elems)], 1, whole)

    def prepare_backward():
        @pl.when(has_right)
        def _():
            halo_copy(halfp, 0, 2, right_dev).start()
            halo_copy(halfp, 1, 3, left_dev).wait_recv()

        halfp[pl.ds(elems + GROUP, GROUP)] = halo[3]
        later = pl.ds(GROUP, elems - GROUP)
        fix[1, later] = (
            fix[1, later]
            - couple(halfp[pl.ds(2 * GROUP - 1, elems - GROUP)], 2, later)
            - couple(halfp[pl.ds(2 * GROUP + 1, elems - GROUP)], 3, later)
        )

    def prepare_first_group():
        @pl.when(has_left)
        def _():
            halo_copy(halfp, 0, 2, right_dev).wait_recv()

        halfp[pl.ds(0, GROUP)] = halo[2]
        first = pl.ds(0, GROUP)
        fix[1, first] = (
            fix[1, first]
            - couple(halfp[pl.ds(GROUP - 1, GROUP)], 2, first)
            - couple(halfp[pl.ds(GROUP + 1, GROUP)], 3, first)
        )

    def half_copy():
        return pltpu.make_async_copy(result.at[0, pl.ds(GROUP, elems)], half_hbm.at[0], out_sem.at[blocks])

    def full_copy(j):
        return pltpu.make_async_copy(result.at[1, padded_rows(j)], full_hbm.at[0, rows(j)], out_sem.at[j])

    def step(t, carry):
        phase = t // blocks
        u = t % blocks
        j = phase * (blocks - 1) + (1 - 2 * phase) * u
        slot = phase * blocks + j
        forward = phase == 0
        backward = phase == 1

        @pl.when(t == blocks)
        def _():
            prepare_backward()
            half_copy().start()

            @pl.when(jnp.logical_not(has_down))
            def _():
                coupled_ref[...] = edge

        @pl.when(t == 2 * blocks - 1)
        def _():
            prepare_first_group()

        @pl.when(forward)
        def _():
            a_copy(j).wait()

        @pl.when(jnp.logical_or(jnp.logical_and(forward, has_up), jnp.logical_and(backward, has_down)))
        def _():
            box_copy(slot, up_dev).wait_recv()
            coupled_ref[...] = couple(permuted(inbox[slot][:, :unk], phase, j), phase, rows(j))

        coupled = coupled_ref[...]
        solved = solve(fix[phase, rows(j)] - coupled, j)
        outbox[slot, :, 0:unk] = solved

        @pl.when(jnp.logical_and(forward, has_down))
        def _():
            box_copy(slot, down_dev).start()

        @pl.when(jnp.logical_and(backward, has_up))
        def _():
            box_copy(slot, up_dev).start()

        result[phase, padded_rows(j)] = solved

        @pl.when(forward)
        def _():
            fix[1, rows(j)] = rhs[0, rows(j)] - coupled

        @pl.when(backward)
        def _():
            full_copy(j).start()

        @pl.when(jnp.logical_and(t == 0, has_left))
        def _():
            halo_copy(halfp, 1, 3, left_dev).start()

        return carry

    outbox[...] = jnp.zeros_like(outbox)
    prepare_forward()
    lax.fori_loop(0, 2 * blocks, step, 0)

    def drain(j, carry):
        @pl.when(has_down)
        def _():
            box_copy(j, down_dev).wait_send()

        @pl.when(has_up)
        def _():
            box_copy(blocks + j, up_dev).wait_send()

        full_copy(j).wait()
        return carry

    lax.fori_loop(0, blocks, drain, 0)
    half_copy().wait()

    @pl.when(has_right)
    def _():
        halo_copy(halfp, 0, 2, right_dev).wait_send()

    @pl.when(has_left)
    def _():
        halo_copy(halfp, 1, 3, left_dev).wait_send()


def per_device(
    right_side, old_state, block_inverse, flux_jacobian, face_lift, upstream, downstream, live_counts
):
    layers, elems, unk = right_side.shape
    assert layers == 1 and elems % GROUP == 0
    nf, nc = lax.axis_size("flow"), lax.axis_size("cross")
    nb = unk // NVAR
    wide = -(-unk // 128) * 128
    groups = elems // GROUP
    hbm = pl.BlockSpec(memory_space=pltpu.HBM)
    blocks = elems // GROUP
    jacobian = jnp.transpose(flux_jacobian[0], (2, 1, 0))
    f32 = jnp.float32
    dma = pltpu.SemaphoreType.DMA
    return pl.pallas_call(
        functools.partial(sweep_kernel, nf, nc),
        out_shape=(jax.ShapeDtypeStruct(right_side.shape, f32),) * 2,
        in_specs=[
            hbm, hbm, hbm, hbm, hbm, hbm, hbm, hbm,
        ],
        out_specs=(hbm, hbm),
        scratch_shapes=[
            pltpu.VMEM(right_side.shape, f32),
            pltpu.VMEM(old_state.shape, f32),
            pltpu.VMEM(jacobian.shape, f32),
            pltpu.VMEM(face_lift.shape, f32),
            pltpu.VMEM(upstream.shape, jnp.int32),
            pltpu.VMEM(downstream.shape, jnp.int32),
            pltpu.VMEM(live_counts.shape, jnp.int32),
            pltpu.VMEM((elems, unk, unk), jnp.bfloat16),
            pltpu.VMEM((4, elems, NVAR * wide), f32),
            pltpu.VMEM((4, unk, nb), jnp.bfloat16),
            pltpu.VMEM((elems + 2 * GROUP, unk), f32),
            pltpu.VMEM((2, elems + 2 * GROUP, unk), f32),
            pltpu.VMEM((elems, unk), f32),
            pltpu.VMEM((4, GROUP, unk), f32),
            pltpu.VMEM((2 * blocks, GROUP, wide), f32),
            pltpu.VMEM((2 * blocks, GROUP, wide), f32),
            pltpu.VMEM((2, elems, unk), f32),
            pltpu.VMEM((2, elems, 128), f32),
            pltpu.VMEM((GROUP, unk), f32),
            dma((7,)), dma((blocks + 1,)), dma((groups,)), dma, dma, dma((4,)), dma((4,)),
            dma((2 * blocks,)), dma((2 * blocks,)),
        ],
        compiler_params=pltpu.CompilerParams(
            collective_id=0, has_side_effects=True, vmem_limit_bytes=VMEM_BYTES
        ),
        cost_estimate=pl.CostEstimate(
            flops=4 * elems * unk * unk, bytes_accessed=2 * elems * unk * unk, transcendentals=0
        ),
        name="sweep",
    )(right_side, old_state, block_inverse, jacobian, face_lift, upstream, downstream, live_counts)


def solution(mesh):
    in_specs = (
        P("flow", "cross", None),
        P("flow", "cross", None),
        P("flow", "cross", None, None),
        P("flow", "cross", None, None),
        P(),
        P("flow", "cross"),
        P("flow", "cross"),
        P("flow", "cross"),
    )
    out_specs = (P("flow", "cross", None), P("flow", "cross", None))
    return jax.shard_map(
        per_device, mesh=mesh, in_specs=in_specs, out_specs=out_specs, check_vma=False
    )
```

```python
import functools

import jax
import jax.numpy as jnp
from jax import lax
from jax.experimental import pallas as pl
from jax.experimental.pallas import tpu as pltpu
from jax.sharding import PartitionSpec as P

NVAR = 5
GROUP = 8
VMEM_BYTES = 64 * 1024 * 1024
MESH = pl.DeviceIdType.MESH
CONTRACT_LAST = (((1,), (1,)), ((), ()))
CONTRACT_FIRST = (((0,), (0,)), ((), ()))


def sweep_kernel(
    nf, nc,
    rhs_hbm, old_hbm, ainv, jac_hbm, lift_hbm, up_hbm, down_hbm, cnt_hbm,
    half_hbm, full_hbm,
    rhs, old, jac, lift, up, down, cnt,
    a_vm, jx, lt, oldp, result, down_in, halo, inbox, outbox, fix, rel, live, coupled_ref,
    in_sem, out_sem, a_sem, old_send, old_recv, halo_send, halo_recv, box_send, box_recv,
):
    elems, unk = rhs.shape[1], rhs.shape[2]
    nb = unk // NVAR
    wide = -(-unk // 128) * 128
    groups = elems // GROUP
    blocks = elems // GROUP
    halfp = result.at[0]
    f = lax.axis_index("flow")
    c = lax.axis_index("cross")
    has_up, has_down = f > 0, f < nf - 1
    has_left, has_right = c > 0, c < nc - 1
    up_dev, down_dev = {"flow": f - 1}, {"flow": f + 1}
    left_dev, right_dev = {"cross": c - 1}, {"cross": c + 1}
    neighbours = ((has_up, up_dev), (has_down, down_dev), (has_left, left_dev), (has_right, right_dev))

    def rows(g):
        return pl.ds(pl.multiple_of(g * GROUP, GROUP), GROUP)

    def padded_rows(g):
        return pl.ds(pl.multiple_of(g * GROUP + GROUP, GROUP), GROUP)

    def a_copy(g):
        return pltpu.make_async_copy(ainv.at[0, rows(g)], a_vm.at[rows(g)], a_sem.at[g])

    def remote(src, dst, ssem, rsem, dev):
        return pltpu.make_async_remote_copy(
            src_ref=src, dst_ref=dst, send_sem=ssem, recv_sem=rsem,
            device_id=dev, device_id_type=MESH,
        )

    def old_copy():
        return remote(oldp.at[pl.ds(GROUP, elems)], down_in, old_send, old_recv, up_dev)

    def halo_copy(buf, which, slot, dev):
        start = elems if which == 0 else GROUP
        return remote(buf.at[pl.ds(start, GROUP)], halo.at[slot], halo_send.at[slot], halo_recv.at[slot], dev)

    def box_copy(slot, dev):
        return remote(outbox.at[slot], inbox.at[slot], box_send.at[slot], box_recv.at[slot], dev)

    sources = (old_hbm, cnt_hbm, jac_hbm, lift_hbm, up_hbm, down_hbm, rhs_hbm)
    fetches = [
        pltpu.make_async_copy(src, dst, in_sem.at[i])
        for i, (src, dst) in enumerate(zip(sources, (old, cnt, jac, lift, up, down, rhs)))
    ]
    for fetch in fetches:
        fetch.start()
    for g in range(groups):
        a_copy(g).start()

    barrier = pltpu.get_barrier_semaphore()
    for there, dev in neighbours:
        @pl.when(there)
        def _(dev=dev):
            pl.semaphore_signal(barrier, inc=1, device_id=dev, device_id_type=MESH)

    fetches[0].wait()
    fetches[1].wait()
    count = cnt[...]
    slot = lax.broadcasted_iota(jnp.int32, (elems, unk), 0)
    live[...] = jnp.where(slot < count, 1.0, 0.0)
    oldp[pl.ds(GROUP, elems)] = old[0] * live[...]

    pl.semaphore_wait(barrier, sum(there.astype(jnp.int32) for there, _ in neighbours))

    @pl.when(has_up)
    def _():
        old_copy().start()

    @pl.when(has_right)
    def _():
        halo_copy(oldp, 0, 0, right_dev).start()

    @pl.when(has_left)
    def _():
        halo_copy(oldp, 1, 1, left_dev).start()

    edge = jnp.zeros((GROUP, unk), jnp.float32)

    @pl.when(jnp.logical_not(has_up))
    def _():
        coupled_ref[...] = edge

    @pl.when(jnp.logical_not(has_down))
    def _():
        down_in[...] = jnp.zeros_like(down_in)

    @pl.when(jnp.logical_not(has_left))
    def _():
        halo[0] = edge
        halo[2] = edge

    @pl.when(jnp.logical_not(has_right))
    def _():
        halo[1] = edge
        halo[3] = edge

    for fetch in fetches[2:]:
        fetch.wait()

    square = (elems, elems)
    diagonal = lax.broadcasted_iota(jnp.int32, square, 0) == lax.broadcasted_iota(jnp.int32, square, 1)
    for i, index in enumerate((up, down)):
        local = (index[...] % GROUP).astype(jnp.float32)
        column = jnp.sum(jnp.where(diagonal, jnp.broadcast_to(local, square), 0.0), axis=1, keepdims=True)
        rel[i] = jnp.broadcast_to(column, (elems, unk))

    n2 = NVAR * NVAR
    entry = lax.broadcasted_iota(jnp.int32, (n2, NVAR * wide), 0)
    place = lax.broadcasted_iota(jnp.int32, (n2, NVAR * wide), 1)
    wanted = ((place % wide) // nb) * NVAR + place // wide
    spread_one = jnp.where(entry == wanted, 1.0, 0.0).astype(jnp.bfloat16)
    for d in range(4):
        block = lift[d].astype(jnp.bfloat16)
        lt[d] = jnp.concatenate([block] * NVAR, axis=0)
        values = jac[:, d, :]
        high = values.astype(jnp.bfloat16)
        low = (values - high.astype(jnp.float32)).astype(jnp.bfloat16)
        jx[d] = lax.dot_general(
            high, spread_one, CONTRACT_FIRST, preferred_element_type=jnp.float32
        ) + lax.dot_general(low, spread_one, CONTRACT_FIRST, preferred_element_type=jnp.float32)

    row = lax.broadcasted_iota(jnp.int32, (GROUP, unk), 0)

    def permuted(x, which, g):
        column = rel[which, rows(g)]
        out = jnp.broadcast_to(x[0:1], (GROUP, unk))
        for k in range(1, GROUP):
            out = jnp.where(column == float(k), x[k : k + 1], out)
        return out

    def couple(x, d, where):
        n = x.shape[0]
        stacked = jnp.concatenate([x[:, v * nb : (v + 1) * nb] for v in range(NVAR)], axis=0)
        spread = lax.dot_general(
            stacked.astype(jnp.bfloat16), lt[d], CONTRACT_LAST, preferred_element_type=jnp.float32
        )
        total = None
        for v in range(NVAR):
            term = jx[d, where, v * wide : v * wide + unk] * spread[v * n : (v + 1) * n]
            total = term if total is None else total + term
        return total

    def solve(resid, j):
        flat = resid.astype(jnp.bfloat16)
        out = jnp.zeros((GROUP, unk), jnp.float32)
        for k in range(GROUP):
            product = lax.dot_general(
                flat, a_vm[j * GROUP + k], CONTRACT_LAST, preferred_element_type=jnp.float32
            )
            out = jnp.where(row == k, product, out)
        return out * live[rows(j)]

    def prepare_forward():
        @pl.when(has_left)
        def _():
            halo_copy(oldp, 0, 0, right_dev).wait_recv()

        @pl.when(has_right)
        def _():
            halo_copy(oldp, 1, 1, left_dev).wait_recv()

        oldp[pl.ds(0, GROUP)] = halo[0]
        oldp[pl.ds(elems + GROUP, GROUP)] = halo[1]

        whole = pl.ds(0, elems)
        sides = couple(oldp[pl.ds(GROUP - 1, elems)], 2, whole) + couple(
            oldp[pl.ds(GROUP + 1, elems)], 3, whole
        )

        @pl.when(has_down)
        def _():
            old_copy().wait_recv()

        @pl.when(has_up)
        def _():
            old_copy().wait_send()

        @pl.when(has_right)
        def _():
            halo_copy(oldp, 0, 0, right_dev).wait_send()

        @pl.when(has_left)
        def _():
            halo_copy(oldp, 1, 1, left_dev).wait_send()

        for g in range(groups):
            x = down_in[pl.ds(g * GROUP, GROUP)]
            oldp[pl.ds(g * GROUP, GROUP)] = permuted(x, 1, g)
        fix[0] = rhs[0] - sides - couple(oldp[pl.ds(0, elems)], 1, whole)

    def prepare_backward():
        @pl.when(has_right)
        def _():
            halo_copy(halfp, 0, 2, right_dev).start()
            halo_copy(halfp, 1, 3, left_dev).wait_recv()

        halfp[pl.ds(elems + GROUP, GROUP)] = halo[3]
        later = pl.ds(GROUP, elems - GROUP)
        fix[1, later] = (
            fix[1, later]
            - couple(halfp[pl.ds(2 * GROUP - 1, elems - GROUP)], 2, later)
            - couple(halfp[pl.ds(2 * GROUP + 1, elems - GROUP)], 3, later)
        )

    def prepare_first_group():
        @pl.when(has_left)
        def _():
            halo_copy(halfp, 0, 2, right_dev).wait_recv()

        halfp[pl.ds(0, GROUP)] = halo[2]
        first = pl.ds(0, GROUP)
        fix[1, first] = (
            fix[1, first]
            - couple(halfp[pl.ds(GROUP - 1, GROUP)], 2, first)
            - couple(halfp[pl.ds(GROUP + 1, GROUP)], 3, first)
        )

    def half_copy():
        return pltpu.make_async_copy(result.at[0, pl.ds(GROUP, elems)], half_hbm.at[0], out_sem.at[blocks])

    def full_copy(j):
        return pltpu.make_async_copy(result.at[1, padded_rows(j)], full_hbm.at[0, rows(j)], out_sem.at[j])

    def step(t, carry):
        phase = t // blocks
        u = t % blocks
        j = phase * (blocks - 1) + (1 - 2 * phase) * u
        slot = phase * blocks + j
        forward = phase == 0
        backward = phase == 1

        @pl.when(t == blocks)
        def _():
            prepare_backward()
            half_copy().start()

            @pl.when(jnp.logical_not(has_down))
            def _():
                coupled_ref[...] = edge

        @pl.when(t == 2 * blocks - 1)
        def _():
            prepare_first_group()

        @pl.when(forward)
        def _():
            a_copy(j).wait()

        @pl.when(jnp.logical_or(jnp.logical_and(forward, has_up), jnp.logical_and(backward, has_down)))
        def _():
            box_copy(slot, up_dev).wait_recv()
            coupled_ref[...] = couple(permuted(inbox[slot][:, :unk], phase, j), phase, rows(j))

        coupled = coupled_ref[...]
        solved = solve(fix[phase, rows(j)] - coupled, j)
        outbox[slot, :, 0:unk] = solved

        @pl.when(jnp.logical_and(forward, has_down))
        def _():
            box_copy(slot, down_dev).start()

        @pl.when(jnp.logical_and(backward, has_up))
        def _():
            box_copy(slot, up_dev).start()

        result[phase, padded_rows(j)] = solved

        @pl.when(forward)
        def _():
            fix[1, rows(j)] = rhs[0, rows(j)] - coupled

        @pl.when(backward)
        def _():
            full_copy(j).start()

        @pl.when(jnp.logical_and(t == 0, has_left))
        def _():
            halo_copy(halfp, 1, 3, left_dev).start()

        return carry

    outbox[...] = jnp.zeros_like(outbox)
    prepare_forward()
    lax.fori_loop(0, 2 * blocks, step, 0)

    def drain(j, carry):
        @pl.when(has_down)
        def _():
            box_copy(j, down_dev).wait_send()

        @pl.when(has_up)
        def _():
            box_copy(blocks + j, up_dev).wait_send()

        full_copy(j).wait()
        return carry

    lax.fori_loop(0, blocks, drain, 0)
    half_copy().wait()

    @pl.when(has_right)
    def _():
        halo_copy(halfp, 0, 2, right_dev).wait_send()

    @pl.when(has_left)
    def _():
        halo_copy(halfp, 1, 3, left_dev).wait_send()


def per_device(
    right_side, old_state, block_inverse, flux_jacobian, face_lift, upstream, downstream, live_counts
):
    layers, elems, unk = right_side.shape
    assert layers == 1 and elems % GROUP == 0
    nf, nc = lax.axis_size("flow"), lax.axis_size("cross")
    nb = unk // NVAR
    wide = -(-unk // 128) * 128
    groups = elems // GROUP
    hbm = pl.BlockSpec(memory_space=pltpu.HBM)
    blocks = elems // GROUP
    jacobian = jnp.transpose(flux_jacobian[0], (2, 1, 0))
    f32 = jnp.float32
    dma = pltpu.SemaphoreType.DMA
    return pl.pallas_call(
        functools.partial(sweep_kernel, nf, nc),
        out_shape=(jax.ShapeDtypeStruct(right_side.shape, f32),) * 2,
        in_specs=[
            hbm, hbm, hbm, hbm, hbm, hbm, hbm, hbm,
        ],
        out_specs=(hbm, hbm),
        scratch_shapes=[
            pltpu.VMEM(right_side.shape, f32),
            pltpu.VMEM(old_state.shape, f32),
            pltpu.VMEM(jacobian.shape, f32),
            pltpu.VMEM(face_lift.shape, f32),
            pltpu.VMEM(upstream.shape, jnp.int32),
            pltpu.VMEM(downstream.shape, jnp.int32),
            pltpu.VMEM(live_counts.shape, jnp.int32),
            pltpu.VMEM((elems, unk, unk), jnp.bfloat16),
            pltpu.VMEM((4, elems, NVAR * wide), f32),
            pltpu.VMEM((4, unk, nb), jnp.bfloat16),
            pltpu.VMEM((elems + 2 * GROUP, unk), f32),
            pltpu.VMEM((2, elems + 2 * GROUP, unk), f32),
            pltpu.VMEM((elems, unk), f32),
            pltpu.VMEM((4, GROUP, unk), f32),
            pltpu.VMEM((2 * blocks, GROUP, wide), f32),
            pltpu.VMEM((2 * blocks, GROUP, wide), f32),
            pltpu.VMEM((2, elems, unk), f32),
            pltpu.VMEM((2, elems, unk), f32),
            pltpu.VMEM((elems, unk), f32),
            pltpu.VMEM((GROUP, unk), f32),
            dma((7,)), dma((blocks + 1,)), dma((groups,)), dma, dma, dma((4,)), dma((4,)),
            dma((2 * blocks,)), dma((2 * blocks,)),
        ],
        compiler_params=pltpu.CompilerParams(
            collective_id=0, has_side_effects=True, vmem_limit_bytes=VMEM_BYTES
        ),
        cost_estimate=pl.CostEstimate(
            flops=4 * elems * unk * unk, bytes_accessed=2 * elems * unk * unk, transcendentals=0
        ),
        name="sweep",
    )(right_side, old_state, block_inverse, jacobian, face_lift, upstream, downstream, live_counts)


def solution(mesh):
    in_specs = (
        P("flow", "cross", None),
        P("flow", "cross", None),
        P("flow", "cross", None, None),
        P("flow", "cross", None, None),
        P(),
        P("flow", "cross"),
        P("flow", "cross"),
        P("flow", "cross"),
    )
    out_specs = (P("flow", "cross", None), P("flow", "cross", None))
    return jax.shard_map(
        per_device, mesh=mesh, in_specs=in_specs, out_specs=out_specs, check_vma=False
    )
```

```python
import functools

import jax
import jax.numpy as jnp
from jax import lax
from jax.experimental import pallas as pl
from jax.experimental.pallas import tpu as pltpu
from jax.sharding import PartitionSpec as P

NVAR = 5
GROUP = 8
VMEM_BYTES = 64 * 1024 * 1024
MESH = pl.DeviceIdType.MESH
CONTRACT_LAST = (((1,), (1,)), ((), ()))
CONTRACT_FIRST = (((0,), (0,)), ((), ()))


def sweep_kernel(
    nf, nc,
    rhs_hbm, old_hbm, ainv, jac_hbm, lift_hbm, up_hbm, down_hbm, cnt_hbm,
    half_hbm, full_hbm,
    rhs, old, jac, lift, up, down, cnt,
    a_vm, jx, lt, oldp, result, down_in, halo, inbox, outbox, fix, rel, live, coupled_ref, packed,
    in_sem, out_sem, a_sem, old_send, old_recv, halo_send, halo_recv, box_send, box_recv,
):
    elems, unk = rhs.shape[1], rhs.shape[2]
    nb = unk // NVAR
    wide = -(-unk // 128) * 128
    groups = elems // GROUP
    blocks = elems // GROUP
    halfp = result.at[0]
    main = unk - unk // NVAR
    rest = unk - main
    f = lax.axis_index("flow")
    c = lax.axis_index("cross")
    has_up, has_down = f > 0, f < nf - 1
    has_left, has_right = c > 0, c < nc - 1
    up_dev, down_dev = {"flow": f - 1}, {"flow": f + 1}
    left_dev, right_dev = {"cross": c - 1}, {"cross": c + 1}
    neighbours = ((has_up, up_dev), (has_down, down_dev), (has_left, left_dev), (has_right, right_dev))

    def rows(g):
        return pl.ds(pl.multiple_of(g * GROUP, GROUP), GROUP)

    def padded_rows(g):
        return pl.ds(pl.multiple_of(g * GROUP + GROUP, GROUP), GROUP)

    def a_copy(g):
        return pltpu.make_async_copy(ainv.at[0, rows(g)], a_vm.at[rows(g)], a_sem.at[g])

    def remote(src, dst, ssem, rsem, dev):
        return pltpu.make_async_remote_copy(
            src_ref=src, dst_ref=dst, send_sem=ssem, recv_sem=rsem,
            device_id=dev, device_id_type=MESH,
        )

    def old_copy():
        return remote(oldp.at[pl.ds(GROUP, elems)], down_in, old_send, old_recv, up_dev)

    def halo_copy(buf, which, slot, dev):
        start = elems if which == 0 else GROUP
        return remote(buf.at[pl.ds(start, GROUP)], halo.at[slot], halo_send.at[slot], halo_recv.at[slot], dev)

    def box_copy(slot, dev):
        return remote(outbox.at[slot], inbox.at[slot], box_send.at[slot], box_recv.at[slot], dev)

    sources = (old_hbm, cnt_hbm, jac_hbm, lift_hbm, up_hbm, down_hbm, rhs_hbm)
    fetches = [
        pltpu.make_async_copy(src, dst, in_sem.at[i])
        for i, (src, dst) in enumerate(zip(sources, (old, cnt, jac, lift, up, down, rhs)))
    ]
    for fetch in fetches:
        fetch.start()
    for g in range(groups):
        a_copy(g).start()

    barrier = pltpu.get_barrier_semaphore()
    for there, dev in neighbours:
        @pl.when(there)
        def _(dev=dev):
            pl.semaphore_signal(barrier, inc=1, device_id=dev, device_id_type=MESH)

    fetches[0].wait()
    fetches[1].wait()
    count = cnt[...]
    slot = lax.broadcasted_iota(jnp.int32, (elems, unk), 0)
    live[...] = jnp.where(slot < count, 1.0, 0.0)
    oldp[pl.ds(GROUP, elems)] = old[0] * live[...]

    pl.semaphore_wait(barrier, sum(there.astype(jnp.int32) for there, _ in neighbours))

    @pl.when(has_up)
    def _():
        old_copy().start()

    @pl.when(has_right)
    def _():
        halo_copy(oldp, 0, 0, right_dev).start()

    @pl.when(has_left)
    def _():
        halo_copy(oldp, 1, 1, left_dev).start()

    edge = jnp.zeros((GROUP, unk), jnp.float32)

    @pl.when(jnp.logical_not(has_up))
    def _():
        coupled_ref[...] = edge

    @pl.when(jnp.logical_not(has_down))
    def _():
        down_in[...] = jnp.zeros_like(down_in)

    @pl.when(jnp.logical_not(has_left))
    def _():
        halo[0] = edge
        halo[2] = edge

    @pl.when(jnp.logical_not(has_right))
    def _():
        halo[1] = edge
        halo[3] = edge

    for fetch in fetches[2:]:
        fetch.wait()

    square = (elems, elems)
    diagonal = lax.broadcasted_iota(jnp.int32, square, 0) == lax.broadcasted_iota(jnp.int32, square, 1)
    for i, index in enumerate((up, down)):
        local = (index[...] % GROUP).astype(jnp.float32)
        column = jnp.sum(jnp.where(diagonal, jnp.broadcast_to(local, square), 0.0), axis=1, keepdims=True)
        rel[i] = jnp.broadcast_to(column, (elems, unk))

    n2 = NVAR * NVAR
    entry = lax.broadcasted_iota(jnp.int32, (n2, NVAR * wide), 0)
    place = lax.broadcasted_iota(jnp.int32, (n2, NVAR * wide), 1)
    wanted = ((place % wide) // nb) * NVAR + place // wide
    spread_one = jnp.where(entry == wanted, 1.0, 0.0).astype(jnp.bfloat16)
    for d in range(4):
        block = lift[d].astype(jnp.bfloat16)
        lt[d] = jnp.concatenate([block] * NVAR, axis=0)
        values = jac[:, d, :]
        high = values.astype(jnp.bfloat16)
        low = (values - high.astype(jnp.float32)).astype(jnp.bfloat16)
        jx[d] = lax.dot_general(
            high, spread_one, CONTRACT_FIRST, preferred_element_type=jnp.float32
        ) + lax.dot_general(low, spread_one, CONTRACT_FIRST, preferred_element_type=jnp.float32)

    row = lax.broadcasted_iota(jnp.int32, (GROUP, unk), 0)

    def permuted(x, which, g):
        column = rel[which, rows(g)]
        out = jnp.broadcast_to(x[0:1], (GROUP, unk))
        for k in range(1, GROUP):
            out = jnp.where(column == float(k), x[k : k + 1], out)
        return out

    def couple(x, d, where):
        n = x.shape[0]
        stacked = jnp.concatenate([x[:, v * nb : (v + 1) * nb] for v in range(NVAR)], axis=0)
        spread = lax.dot_general(
            stacked.astype(jnp.bfloat16), lt[d], CONTRACT_LAST, preferred_element_type=jnp.float32
        )
        total = None
        for v in range(NVAR):
            term = jx[d, where, v * wide : v * wide + unk] * spread[v * n : (v + 1) * n]
            total = term if total is None else total + term
        return total

    def solve(resid, j):
        tail = jnp.concatenate([resid[:, main:]] * GROUP, axis=1)
        lane = lax.broadcasted_iota(jnp.int32, (GROUP, GROUP * rest), 1)
        line = lax.broadcasted_iota(jnp.int32, (GROUP, GROUP * rest), 0)
        tail = jnp.where(lane // rest == line, tail, 0.0).astype(jnp.bfloat16)
        head = resid[:, :main].astype(jnp.bfloat16)
        out = jnp.zeros((GROUP, unk), jnp.float32)
        for k in range(GROUP):
            product = lax.dot_general(
                head, a_vm[j * GROUP + k, :, 0:main], CONTRACT_LAST, preferred_element_type=jnp.float32
            )
            out = jnp.where(row == k, product, out)
        out = out + lax.dot_general(tail, packed[j], CONTRACT_LAST, preferred_element_type=jnp.float32)
        return out * live[rows(j)]

    def pack(j, carry):
        a_copy(j).wait()
        packed[j] = jnp.concatenate([a_vm[j * GROUP + k, :, main:] for k in range(GROUP)], axis=1)
        return carry

    lax.fori_loop(0, blocks, pack, 0)

    def prepare_forward():
        @pl.when(has_left)
        def _():
            halo_copy(oldp, 0, 0, right_dev).wait_recv()

        @pl.when(has_right)
        def _():
            halo_copy(oldp, 1, 1, left_dev).wait_recv()

        oldp[pl.ds(0, GROUP)] = halo[0]
        oldp[pl.ds(elems + GROUP, GROUP)] = halo[1]

        whole = pl.ds(0, elems)
        sides = couple(oldp[pl.ds(GROUP - 1, elems)], 2, whole) + couple(
            oldp[pl.ds(GROUP + 1, elems)], 3, whole
        )

        @pl.when(has_down)
        def _():
            old_copy().wait_recv()

        @pl.when(has_up)
        def _():
            old_copy().wait_send()

        @pl.when(has_right)
        def _():
            halo_copy(oldp, 0, 0, right_dev).wait_send()

        @pl.when(has_left)
        def _():
            halo_copy(oldp, 1, 1, left_dev).wait_send()

        for g in range(groups):
            x = down_in[pl.ds(g * GROUP, GROUP)]
            oldp[pl.ds(g * GROUP, GROUP)] = permuted(x, 1, g)
        fix[0] = rhs[0] - sides - couple(oldp[pl.ds(0, elems)], 1, whole)

    def prepare_backward():
        @pl.when(has_right)
        def _():
            halo_copy(halfp, 0, 2, right_dev).start()
            halo_copy(halfp, 1, 3, left_dev).wait_recv()

        halfp[pl.ds(elems + GROUP, GROUP)] = halo[3]
        later = pl.ds(GROUP, elems - GROUP)
        fix[1, later] = (
            fix[1, later]
            - couple(halfp[pl.ds(2 * GROUP - 1, elems - GROUP)], 2, later)
            - couple(halfp[pl.ds(2 * GROUP + 1, elems - GROUP)], 3, later)
        )

    def prepare_first_group():
        @pl.when(has_left)
        def _():
            halo_copy(halfp, 0, 2, right_dev).wait_recv()

        halfp[pl.ds(0, GROUP)] = halo[2]
        first = pl.ds(0, GROUP)
        fix[1, first] = (
            fix[1, first]
            - couple(halfp[pl.ds(GROUP - 1, GROUP)], 2, first)
            - couple(halfp[pl.ds(GROUP + 1, GROUP)], 3, first)
        )

    def half_copy():
        return pltpu.make_async_copy(result.at[0, pl.ds(GROUP, elems)], half_hbm.at[0], out_sem.at[blocks])

    def full_copy(j):
        return pltpu.make_async_copy(result.at[1, padded_rows(j)], full_hbm.at[0, rows(j)], out_sem.at[j])

    def step(t, carry):
        phase = t // blocks
        u = t % blocks
        j = phase * (blocks - 1) + (1 - 2 * phase) * u
        slot = phase * blocks + j
        forward = phase == 0
        backward = phase == 1

        @pl.when(t == blocks)
        def _():
            prepare_backward()
            half_copy().start()

            @pl.when(jnp.logical_not(has_down))
            def _():
                coupled_ref[...] = edge

        @pl.when(t == 2 * blocks - 1)
        def _():
            prepare_first_group()

        @pl.when(jnp.logical_or(jnp.logical_and(forward, has_up), jnp.logical_and(backward, has_down)))
        def _():
            box_copy(slot, up_dev).wait_recv()
            coupled_ref[...] = couple(permuted(inbox[slot][:, :unk], phase, j), phase, rows(j))

        coupled = coupled_ref[...]
        solved = solve(fix[phase, rows(j)] - coupled, j)
        outbox[slot, :, 0:unk] = solved

        @pl.when(jnp.logical_and(forward, has_down))
        def _():
            box_copy(slot, down_dev).start()

        @pl.when(jnp.logical_and(backward, has_up))
        def _():
            box_copy(slot, up_dev).start()

        result[phase, padded_rows(j)] = solved

        @pl.when(forward)
        def _():
            fix[1, rows(j)] = rhs[0, rows(j)] - coupled

        @pl.when(backward)
        def _():
            full_copy(j).start()

        @pl.when(jnp.logical_and(t == 0, has_left))
        def _():
            halo_copy(halfp, 1, 3, left_dev).start()

        return carry

    outbox[...] = jnp.zeros_like(outbox)
    prepare_forward()
    lax.fori_loop(0, 2 * blocks, step, 0)

    def drain(j, carry):
        @pl.when(has_down)
        def _():
            box_copy(j, down_dev).wait_send()

        @pl.when(has_up)
        def _():
            box_copy(blocks + j, up_dev).wait_send()

        full_copy(j).wait()
        return carry

    lax.fori_loop(0, blocks, drain, 0)
    half_copy().wait()

    @pl.when(has_right)
    def _():
        halo_copy(halfp, 0, 2, right_dev).wait_send()

    @pl.when(has_left)
    def _():
        halo_copy(halfp, 1, 3, left_dev).wait_send()


def per_device(
    right_side, old_state, block_inverse, flux_jacobian, face_lift, upstream, downstream, live_counts
):
    layers, elems, unk = right_side.shape
    assert layers == 1 and elems % GROUP == 0
    nf, nc = lax.axis_size("flow"), lax.axis_size("cross")
    nb = unk // NVAR
    wide = -(-unk // 128) * 128
    groups = elems // GROUP
    hbm = pl.BlockSpec(memory_space=pltpu.HBM)
    blocks = elems // GROUP
    jacobian = jnp.transpose(flux_jacobian[0], (2, 1, 0))
    f32 = jnp.float32
    dma = pltpu.SemaphoreType.DMA
    return pl.pallas_call(
        functools.partial(sweep_kernel, nf, nc),
        out_shape=(jax.ShapeDtypeStruct(right_side.shape, f32),) * 2,
        in_specs=[
            hbm, hbm, hbm, hbm, hbm, hbm, hbm, hbm,
        ],
        out_specs=(hbm, hbm),
        scratch_shapes=[
            pltpu.VMEM(right_side.shape, f32),
            pltpu.VMEM(old_state.shape, f32),
            pltpu.VMEM(jacobian.shape, f32),
            pltpu.VMEM(face_lift.shape, f32),
            pltpu.VMEM(upstream.shape, jnp.int32),
            pltpu.VMEM(downstream.shape, jnp.int32),
            pltpu.VMEM(live_counts.shape, jnp.int32),
            pltpu.VMEM((elems, unk, unk), jnp.bfloat16),
            pltpu.VMEM((4, elems, NVAR * wide), f32),
            pltpu.VMEM((4, unk, nb), jnp.bfloat16),
            pltpu.VMEM((elems + 2 * GROUP, unk), f32),
            pltpu.VMEM((2, elems + 2 * GROUP, unk), f32),
            pltpu.VMEM((elems, unk), f32),
            pltpu.VMEM((4, GROUP, unk), f32),
            pltpu.VMEM((2 * blocks, GROUP, wide), f32),
            pltpu.VMEM((2 * blocks, GROUP, wide), f32),
            pltpu.VMEM((2, elems, unk), f32),
            pltpu.VMEM((2, elems, unk), f32),
            pltpu.VMEM((elems, unk), f32),
            pltpu.VMEM((GROUP, unk), f32),
            pltpu.VMEM((blocks, unk, GROUP * (unk // NVAR)), jnp.bfloat16),
            dma((7,)), dma((blocks + 1,)), dma((groups,)), dma, dma, dma((4,)), dma((4,)),
            dma((2 * blocks,)), dma((2 * blocks,)),
        ],
        compiler_params=pltpu.CompilerParams(
            collective_id=0, has_side_effects=True, vmem_limit_bytes=VMEM_BYTES
        ),
        cost_estimate=pl.CostEstimate(
            flops=4 * elems * unk * unk, bytes_accessed=2 * elems * unk * unk, transcendentals=0
        ),
        name="sweep",
    )(right_side, old_state, block_inverse, jacobian, face_lift, upstream, downstream, live_counts)


def solution(mesh):
    in_specs = (
        P("flow", "cross", None),
        P("flow", "cross", None),
        P("flow", "cross", None, None),
        P("flow", "cross", None, None),
        P(),
        P("flow", "cross"),
        P("flow", "cross"),
        P("flow", "cross"),
    )
    out_specs = (P("flow", "cross", None), P("flow", "cross", None))
    return jax.shard_map(
        per_device, mesh=mesh, in_specs=in_specs, out_specs=out_specs, check_vma=False
    )
```
